32 devices in a mesh: groups: 2 (over y), wide: 4 (over z), narrow: 2 (over x), aux: 2 (over core).
Axes of the slice: x: 2, y: 2, z: 4, core: 2. Of those that a mesh axis runs over, the one named last changes fastest.
Arguments:
- dissimilarity: bfloat16 [10240, 5120], P(('groups', 'narrow', 'aux'), 'wide'), parts along dimension 0, may hold values from 0 to 37.5, as said below
- config: float32 [10240, 64], P(('groups', 'narrow', 'aux')), parts along dimension 0, may hold values from -8 to 8
Outputs:
- embedding: float32 [10240, 64], P(('groups', 'narrow', 'aux')), parts along dimension 0
- stress: float32 [2], P('groups'), parts along dimension 0
The draws below stay inside these ranges and needn't reach their ends.
There are 2 independent parts, one for each index of `groups`. The reference program is written for one: setup_inputs(seed, part) draws one part's arguments, and reference() takes and returns one part's arrays. A program takes and returns all parts, laid end to end along the dimension named above; each array names one. Nothing has to cross between parts.
Inputs may be any that keep to these rules, and one draw needn't show every extreme that they name: `dissimilarity`: Symmetric, zero on the diagonal, positive off it.
All inputs are finite; a program needn't handle non-finite values.
Results may differ from the reference program's by a relative error of at most 0.0003.
Values sent between devices are 32-bit elements; how exact they have to be, the bound alone decides.
No kernel may reach another device: no remote copies, remote signals or barrier semaphores. Data moves between devices by JAX's collectives and lax.ppermute only.
A program may use at most 64 MiB of HBM per device.

```python
import jax
import jax.numpy as jnp
from jax import lax

P_SIZE = 64
TILE = 1280
ITERS = 2
NPTS = 5120


def draw_dissimilarity(key, part):
    key = jax.random.fold_in(key, 11)
    factor_key, jitter_key = jax.random.split(key)
    factors = jnp.exp(jax.random.uniform(factor_key, (NPTS,), jnp.float32, 0.0, jnp.log(5.0)))
    jitter = jax.random.uniform(jitter_key, (NPTS, NPTS), jnp.float32, 0.5, 1.5)
    symmetric = 0.5 * (jitter + jitter.T)
    values = factors[:, None] * factors[None, :] * symmetric
    positions = jnp.arange(NPTS)
    values = jnp.where(positions[:, None] == positions[None, :], 0.0, values)
    return values.astype(jnp.bfloat16)


def draw_config(key, part):
    key = jax.random.fold_in(key, 23)
    spread_key, base_key = jax.random.split(key)
    spread = jnp.exp(jax.random.uniform(spread_key, (NPTS, 1), jnp.float32, jnp.log(0.2), jnp.log(2.0)))
    base = jnp.clip(jax.random.normal(base_key, (NPTS, P_SIZE), jnp.float32), -4.0, 4.0)
    return (spread * base).astype(jnp.float32)


def setup_inputs(seed: int = 0, part: int = 0) -> dict:
    arg_keys = jax.random.split(jax.random.key(seed), 3)
    part_keys = jax.random.split(jax.random.fold_in(arg_keys[2], part), 3)
    dissimilarity = draw_dissimilarity(jax.random.fold_in(jax.random.fold_in(arg_keys[2], part), 71), part)
    config = draw_config(jax.random.fold_in(jax.random.fold_in(arg_keys[2], part), 71), part)
    return {"dissimilarity": dissimilarity, "config": config}


floor_dist = 3.0

def tile_terms(dissim_tile, own_rows, far_rows):
    own_sq = lax.optimization_barrier(jnp.sum(own_rows * own_rows, axis=1))
    far_sq = lax.optimization_barrier(jnp.sum(far_rows * far_rows, axis=1))
    products = jnp.einsum('ip,jp->ij', own_rows, far_rows, precision=lax.Precision.HIGHEST)
    squared = own_sq[:, None] + far_sq[None, :] - 2.0 * products
    distance = jnp.sqrt(jnp.maximum(squared, 0.0))
    ratios = dissim_tile / jnp.maximum(distance, floor_dist)
    guttman = own_rows * lax.optimization_barrier(jnp.sum(ratios, axis=1))[:, None] - jnp.dot(ratios, far_rows, precision=lax.Precision.HIGHEST)
    misfit = jnp.sum((dissim_tile - distance) ** 2)
    norm_sum = jnp.sum(dissim_tile * dissim_tile)
    return (guttman, misfit, norm_sum)

def reference(dissimilarity, config):
    points = dissimilarity.shape[0]
    blocks = points // TILE
    current = config
    misfits = None
    norm_sums = None
    for iteration in range(ITERS):

        def one_block(block_index, current=current):
            offset = block_index * TILE
            dissim_tile = lax.dynamic_slice_in_dim(dissimilarity, offset, TILE, 0).astype(jnp.float32)
            own_rows = lax.dynamic_slice_in_dim(current, offset, TILE, 0)
            return tile_terms(dissim_tile, own_rows, current)
        guttman, misfits, norm_sums = lax.map(one_block, jnp.arange(blocks, dtype=jnp.int32))
        current = guttman.reshape(points, config.shape[1]) / points
    return (current, (jnp.sum(misfits) / jnp.sum(norm_sums)).reshape(1))
```

```python
import functools

import jax
import jax.numpy as jnp
from jax import lax
from jax.experimental import pallas as pl
from jax.experimental.pallas import tpu as pltpu
from jax.sharding import PartitionSpec as P

ITERS = 2
FLOOR = 3.0
TINY = 1e-30
DEPTH = 256
LANES = 128
EXTRA = 16
SUMS = 16

f32 = jnp.float32
bf16 = jnp.bfloat16
AXES = ("wide", "narrow", "aux")


def split2(values):
    high = values.astype(bf16)
    return high, (values - high.astype(f32)).astype(bf16)


def split3(values):
    high = values.astype(bf16)
    rest = values - high.astype(f32)
    middle = rest.astype(bf16)
    return high, middle, (rest - middle.astype(f32)).astype(bf16)


def norm_rows(points, first):
    count = points.shape[1]
    squares = jnp.sum(points * points, axis=0, keepdims=True)
    row = lax.broadcasted_iota(jnp.int32, (EXTRA, count), 0)
    ones = 3 if first else 0
    parts = 0 if first else 3
    rows = jnp.where((row >= ones) & (row < ones + 3), 1.0, 0.0)
    for k, part in enumerate(split3(squares)):
        rows = jnp.where(row == parts + k, part.astype(f32), rows)
    return rows.astype(bf16)


def tile_body(scale, stress, row_step, col_step, load, delta_ref, norm_ref, *refs):
    (keep_ref, send_ref, row_pts, col_pts, result, lhs, rhs, left, r_high, r_low) = refs[-10:]
    load(refs[:-10], row_pts, col_pts)
    dims, rows = row_pts.shape
    cols = col_pts.shape[1]
    points = row_pts[...]
    high, middle, low = split3(points)
    minus2 = lambda v: (v.astype(f32) * -2.0).astype(bf16)
    fill = DEPTH - 3 * dims - EXTRA
    lhs[...] = jnp.concatenate(
        [minus2(high), minus2(high), minus2(middle), norm_rows(points, True), jnp.zeros((fill, rows), bf16)], axis=0
    ).T
    left[...] = jnp.concatenate([high, middle, low, jnp.ones((EXTRA, rows), bf16)], axis=0)
    points = col_pts[...]
    high, middle = split2(points)
    rhs[...] = jnp.concatenate(
        [high, middle, high, norm_rows(points, False), jnp.zeros((fill, cols), bf16)], axis=0
    )
    misfit = jnp.zeros((8, LANES), f32)
    for jc in range(cols // col_step):
        js = pl.ds(jc * col_step, col_step)
        slot = jc % 2
        for ic in range(rows // row_step):
            rs = pl.ds(ic * row_step, row_step)
            squared = jnp.dot(lhs[rs, :], rhs[:, js], preferred_element_type=f32)
            delta = delta_ref[rs, js].astype(f32)
            if stress:
                inverse = lax.rsqrt(jnp.maximum(squared, TINY))
                ratio = delta * jnp.minimum(inverse, 1.0 / FLOOR)
                gap = delta - jnp.maximum(squared, 0.0) * inverse
                gap = gap * gap
                for c in range(col_step // LANES):
                    part = gap[:, c * LANES:(c + 1) * LANES]
                    misfit = misfit + jnp.sum(part.reshape(row_step // 8, 8, LANES), axis=0)
            else:
                ratio = delta * lax.rsqrt(jnp.maximum(squared, FLOOR * FLOOR))
            high, low = split2(ratio)
            r_high[slot, rs, :] = high
            r_low[slot, rs, :] = low
        terms = jnp.dot(left[...], r_high[slot], preferred_element_type=f32)
        terms = terms + jnp.dot(left[...], r_low[slot], preferred_element_type=f32)
        cross = terms[:dims] + terms[dims:2 * dims] + terms[2 * dims:3 * dims]
        result[:, js] = (col_pts[:, js] * terms[3 * dims:3 * dims + 1] - cross) * scale
    half = dims // 2
    mine = lax.axis_index("aux")
    for ref, which in ((keep_ref, mine), (send_ref, 1 - mine)):
        ref[:, :cols] = result[pl.ds(pl.multiple_of(which * half, 8), half), :]
        if stress:
            ref[:8, cols:] = misfit
            ref[8:16, cols:] = norm_ref[...]
            ref[16:, cols:] = jnp.zeros((half - 16, LANES), f32)


def tile_call(load, scale, stress, dims, delta, norm, *arrays):
    rows, cols = delta.shape
    wide = cols + (LANES if stress else 0)
    step = 256 if rows % 256 == 0 and cols % 256 == 0 else 128
    vmem = pl.BlockSpec(memory_space=pltpu.VMEM)
    out = jax.ShapeDtypeStruct((dims // 2, wide), f32)
    return pl.pallas_call(
        functools.partial(tile_body, scale, stress, step, step, load),
        out_shape=(out, out),
        in_specs=[vmem] * (2 + len(arrays)),
        out_specs=(vmem, vmem),
        scratch_shapes=[
            pltpu.VMEM((dims, rows), f32),
            pltpu.VMEM((dims, cols), f32),
            pltpu.VMEM((dims, cols), f32),
            pltpu.VMEM((rows, DEPTH), bf16),
            pltpu.VMEM((DEPTH, cols), bf16),
            pltpu.VMEM((3 * dims + EXTRA, rows), bf16),
            pltpu.VMEM((2, rows, step), bf16),
            pltpu.VMEM((2, rows, step), bf16),
        ],
        compiler_params=pltpu.CompilerParams(vmem_limit_bytes=40 << 20),
        name="tile",
    )(delta, norm, *arrays)


def norm_body(delta_ref, out_ref):
    rows, cols = delta_ref.shape
    total = jnp.zeros((8, LANES), f32)
    for ic in range(rows // LANES):
        for jc in range(cols // LANES):
            part = delta_ref[ic * LANES:(ic + 1) * LANES, jc * LANES:(jc + 1) * LANES].astype(f32)
            total = total + jnp.sum((part * part).reshape(LANES // 8, 8, LANES), axis=0)
    out_ref[...] = total


def norm_call(delta):
    vmem = pl.BlockSpec(memory_space=pltpu.VMEM)
    return pl.pallas_call(
        norm_body,
        out_shape=jax.ShapeDtypeStruct((8, LANES), f32),
        in_specs=[vmem],
        out_specs=vmem,
        compiler_params=pltpu.CompilerParams(vmem_limit_bytes=40 << 20),
        name="norm",
    )(delta)


class Grid:
    def __init__(self):
        self.narrow = lax.axis_size("narrow")
        self.wide = lax.axis_size("wide")
        self.x = lax.axis_index("narrow")
        self.a = lax.axis_index("aux")
        self.z = lax.axis_index("wide")
        assert lax.axis_size("aux") == 2 and self.wide == 2 * self.narrow

    def pairs(self, source):
        place = lambda x, a, z: (z * self.narrow + x) * 2 + a
        return [
            (place(*source(x, a, z)), place(x, a, z))
            for z in range(self.wide)
            for x in range(self.narrow)
            for a in range(2)
        ]

    def send(self, value, source):
        return lax.ppermute(value, AXES, self.pairs(source))

    def other_core(self, value):
        return lax.ppermute(value, "aux", [(0, 1), (1, 0)])

    def across(self, value, axis, bit):
        return lax.ppermute(value, axis, [(i, i ^ bit) for i in range(lax.axis_size(axis))])

    def spread(self, first):
        def source(x, a, z):
            block = 2 * x + a
            offset = z ^ block
            top, low = offset // self.narrow, offset % self.narrow
            if first:
                return x ^ low, a ^ (1 - top), block
            return x ^ low ^ (1 - top), a ^ top, block

        return source

    def spread_half(self):
        top = (self.z ^ (2 * self.x + self.a)) // self.narrow
        return self.a ^ (1 - top)


def bits(count):
    return [1 << k for k in range(count.bit_length() - 1)]


def first_columns(grid, own):
    x_home = lambda z: z // 2
    current = own
    steps = bits(grid.narrow)
    for place, bit in enumerate(reversed(steps)):

        def source(x, a, z):
            return (x ^ bit, a, z) if a == z % 2 else (x, 1 - a, z ^ 1)

        got = grid.send(current, source)
        if place < len(steps) - 1:
            rest = (grid.x ^ (grid.z // 2)) & (2 * bit - 1)
            current = jnp.where((rest == bit) & (grid.a == grid.z % 2), got, current)
        elif len(steps) > 1:
            rest = (grid.x ^ (grid.z // 2)) & (2 * bit - 1)
            got = jnp.where(rest == bit, got, current)
    return got, grid.other_core(got)


def load_first(narrow, refs, row_pts, col_pts):
    own, got, passed = refs
    x, a, z = (lax.axis_index(n) for n in ("narrow", "aux", "wide"))
    home = (x == z // 2) & (narrow == 2)
    core = a == z % 2
    row_pts[...] = own[...]

    @pl.when(home & core)
    def _():
        col_pts[...] = own[...]

    @pl.when(home != core)
    def _():
        col_pts[...] = got[...]

    @pl.when(jnp.logical_not(home | core))
    def _():
        col_pts[...] = passed[...]


def load_next(narrow, refs, row_pts, col_pts):
    kept, passed, first, second = refs
    x, a, z = (lax.axis_index(n) for n in ("narrow", "aux", "wide"))
    half = kept.shape[0]
    top = (z ^ (2 * x + a)) // narrow
    side = a ^ (1 - top)
    at = lambda which: pl.ds(pl.multiple_of(which * half, 8), half)
    col_pts[at(a), :] = kept[...]
    col_pts[at(1 - a), :] = passed[...]
    row_pts[at(side), :] = first[...]
    row_pts[at(1 - side), :] = second[...]


def shards(dissimilarity, config):
    grid = Grid()
    dims = config.shape[1]
    cols = dissimilarity.shape[1]
    scale = 1.0 / (cols * grid.wide)
    own = config.T
    got, passed = first_columns(grid, own)
    norm = norm_call(dissimilarity)

    keep, send = tile_call(functools.partial(load_first, grid.narrow), scale, False, dims, dissimilarity, norm, own, got, passed)
    for iteration in range(1, ITERS + 1):
        last = iteration == ITERS
        half = keep + grid.other_core(send)
        for bit in bits(grid.narrow):
            half = half + grid.across(half, "narrow", bit)
        part = half[:, :cols]
        first = grid.send(part, grid.spread(True))
        second = grid.send(part, grid.spread(False))
        if last:
            break
        other = grid.other_core(part)
        load = functools.partial(load_next, grid.narrow)
        keep, send = tile_call(
            load, scale, iteration + 1 == ITERS, dims, dissimilarity, norm, part, other, first, second
        )
    sums = half[:SUMS, cols:]
    for bit in bits(grid.wide):
        sums = sums + grid.across(sums, "wide", bit)
    in_order = grid.spread_half() == 0
    embedding = jnp.where(
        in_order, jnp.concatenate([first, second], axis=0), jnp.concatenate([second, first], axis=0)
    )
    stress = jnp.sum(sums[:8]) / jnp.sum(sums[8:])
    return embedding.T, stress.reshape(1)


def solution(mesh):
    placed = (P(("groups", "narrow", "aux"), "wide"), P(("groups", "narrow", "aux"), None))
    return jax.shard_map(
        shards,
        mesh=mesh,
        in_specs=placed,
        out_specs=(P(("groups", "narrow", "aux"), None), P("groups")),
        check_vma=False,
    )
```

```python
import functools

import jax
import jax.numpy as jnp
from jax import lax
from jax.experimental import pallas as pl
from jax.experimental.pallas import tpu as pltpu
from jax.sharding import PartitionSpec as P

ITERS = 2
FLOOR = 3.0
TINY = 1e-30
DEPTH = 256
LANES = 128
EXTRA = 16
SUMS = 16

f32 = jnp.float32
bf16 = jnp.bfloat16
AXES = ("wide", "narrow", "aux")


def split2(values):
    high = values.astype(bf16)
    return high, (values - high.astype(f32)).astype(bf16)


def split3(values):
    high = values.astype(bf16)
    rest = values - high.astype(f32)
    middle = rest.astype(bf16)
    return high, middle, (rest - middle.astype(f32)).astype(bf16)


def norm_rows(points, first):
    count = points.shape[1]
    squares = jnp.sum(points * points, axis=0, keepdims=True)
    row = lax.broadcasted_iota(jnp.int32, (EXTRA, count), 0)
    ones = 3 if first else 0
    parts = 0 if first else 3
    rows = jnp.where((row >= ones) & (row < ones + 3), 1.0, 0.0)
    for k, part in enumerate(split3(squares)):
        rows = jnp.where(row == parts + k, part.astype(f32), rows)
    return rows.astype(bf16)


def tile_body(scale, stress, row_step, col_step, load, delta_ref, norm_ref, *refs):
    (keep_ref, send_ref, row_pts, col_pts, result, lhs, rhs, left, r_high, r_low) = refs[-10:]
    load(refs[:-10], row_pts, col_pts)
    dims, rows = row_pts.shape
    cols = col_pts.shape[1]
    points = row_pts[...]
    high, middle, low = split3(points)
    minus2 = lambda v: (v.astype(f32) * -2.0).astype(bf16)
    fill = DEPTH - 3 * dims - EXTRA
    lhs[...] = jnp.concatenate(
        [minus2(high), minus2(high), minus2(middle), norm_rows(points, True), jnp.zeros((fill, rows), bf16)], axis=0
    ).T
    left[...] = jnp.concatenate([high, middle, low, jnp.ones((EXTRA, rows), bf16)], axis=0)
    points = col_pts[...]
    high, middle = split2(points)
    rhs[...] = jnp.concatenate(
        [high, middle, high, norm_rows(points, False), jnp.zeros((fill, cols), bf16)], axis=0
    )
    misfit = jnp.zeros((8, LANES), f32)
    for jc in range(cols // col_step):
        js = pl.ds(jc * col_step, col_step)
        slot = jc % 2
        for ic in range(rows // row_step):
            rs = pl.ds(ic * row_step, row_step)
            squared = jnp.dot(lhs[rs, :], rhs[:, js], preferred_element_type=f32)
            delta = delta_ref[rs, js].astype(f32)
            if stress:
                inverse = lax.rsqrt(jnp.maximum(squared, TINY))
                ratio = delta * jnp.minimum(inverse, 1.0 / FLOOR)
                gap = delta - jnp.maximum(squared, 0.0) * inverse
                gap = gap * gap
                for c in range(col_step // LANES):
                    part = gap[:, c * LANES:(c + 1) * LANES]
                    misfit = misfit + jnp.sum(part.reshape(row_step // 8, 8, LANES), axis=0)
            else:
                ratio = delta * lax.rsqrt(jnp.maximum(squared, FLOOR * FLOOR))
            high, low = split2(ratio)
            r_high[slot, rs, :] = high
            r_low[slot, rs, :] = low
        terms = jnp.dot(left[...], r_high[slot], preferred_element_type=f32)
        terms = terms + jnp.dot(left[...], r_low[slot], preferred_element_type=f32)
        cross = terms[:dims] + terms[dims:2 * dims] + terms[2 * dims:3 * dims]
        result[:, js] = (col_pts[:, js] * terms[3 * dims:3 * dims + 1] - cross) * scale
    half = dims // 2
    mine = lax.axis_index("aux")
    for ref, which in ((keep_ref, mine), (send_ref, 1 - mine)):
        ref[:, :cols] = result[pl.ds(pl.multiple_of(which * half, 8), half), :]
        if stress:
            ref[:8, cols:] = misfit
            ref[8:16, cols:] = norm_ref[...]
            ref[16:, cols:] = jnp.zeros((half - 16, LANES), f32)


def tile_call(load, scale, stress, dims, delta, norm, *arrays):
    rows, cols = delta.shape
    wide = cols + (LANES if stress else 0)
    step = 256 if rows % 256 == 0 and cols % 256 == 0 else 128
    vmem = pl.BlockSpec(memory_space=pltpu.VMEM)
    out = jax.ShapeDtypeStruct((dims // 2, wide), f32)
    return pl.pallas_call(
        functools.partial(tile_body, scale, stress, step, step, load),
        out_shape=(out, out),
        in_specs=[vmem] * (2 + len(arrays)),
        out_specs=(vmem, vmem),
        scratch_shapes=[
            pltpu.VMEM((dims, rows), f32),
            pltpu.VMEM((dims, cols), f32),
            pltpu.VMEM((dims, cols), f32),
            pltpu.VMEM((rows, DEPTH), bf16),
            pltpu.VMEM((DEPTH, cols), bf16),
            pltpu.VMEM((3 * dims + EXTRA, rows), bf16),
            pltpu.VMEM((2, rows, step), bf16),
            pltpu.VMEM((2, rows, step), bf16),
        ],
        compiler_params=pltpu.CompilerParams(vmem_limit_bytes=40 << 20),
        cost_estimate=pl.CostEstimate(
            flops=2 * 3 * rows * cols * DEPTH, bytes_accessed=2 * rows * cols, transcendentals=rows * cols
        ),
        name="tile",
    )(delta, norm, *arrays)


def norm_body(delta_ref, out_ref):
    rows, cols = delta_ref.shape
    total = jnp.zeros((8, LANES), f32)
    for ic in range(rows // LANES):
        for jc in range(cols // LANES):
            part = delta_ref[ic * LANES:(ic + 1) * LANES, jc * LANES:(jc + 1) * LANES].astype(f32)
            total = total + jnp.sum((part * part).reshape(LANES // 8, 8, LANES), axis=0)
    out_ref[...] = total


def norm_call(delta):
    vmem = pl.BlockSpec(memory_space=pltpu.VMEM)
    return pl.pallas_call(
        norm_body,
        out_shape=jax.ShapeDtypeStruct((8, LANES), f32),
        in_specs=[vmem],
        out_specs=vmem,
        compiler_params=pltpu.CompilerParams(vmem_limit_bytes=40 << 20),
        cost_estimate=pl.CostEstimate(
            flops=4 * delta.size, bytes_accessed=2 * delta.size, transcendentals=0
        ),
        name="norm",
    )(delta)


def stress_body(mine_ref, other_ref, out_ref):
    total = mine_ref[...] + other_ref[...]
    out_ref[0] = jnp.sum(total[:8]) / jnp.sum(total[8:])


def stress_call(mine, other):
    vmem = pl.BlockSpec(memory_space=pltpu.VMEM)
    return pl.pallas_call(
        stress_body,
        out_shape=jax.ShapeDtypeStruct((1,), f32),
        in_specs=[vmem] * 2,
        out_specs=pl.BlockSpec(memory_space=pltpu.SMEM),
        name="stress",
    )(mine, other)


class Grid:
    def __init__(self):
        self.narrow = lax.axis_size("narrow")
        self.wide = lax.axis_size("wide")
        self.x = lax.axis_index("narrow")
        self.a = lax.axis_index("aux")
        self.z = lax.axis_index("wide")
        assert lax.axis_size("aux") == 2 and self.wide == 2 * self.narrow

    def pairs(self, source):
        place = lambda x, a, z: (z * self.narrow + x) * 2 + a
        return [
            (place(*source(x, a, z)), place(x, a, z))
            for z in range(self.wide)
            for x in range(self.narrow)
            for a in range(2)
        ]

    def send(self, value, source):
        return lax.ppermute(value, AXES, self.pairs(source))

    def other_core(self, value):
        return lax.ppermute(value, "aux", [(0, 1), (1, 0)])

    def across(self, value, axis, bit):
        return lax.ppermute(value, axis, [(i, i ^ bit) for i in range(lax.axis_size(axis))])

    def spread(self, first):
        def source(x, a, z):
            block = 2 * x + a
            offset = z ^ block
            top, low = offset // self.narrow, offset % self.narrow
            if first:
                return x ^ low, a ^ (1 - top), block
            return x ^ low ^ (1 - top), a ^ top, block

        return source

    def spread_half(self):
        top = (self.z ^ (2 * self.x + self.a)) // self.narrow
        return self.a ^ (1 - top)


def bits(count):
    return [1 << k for k in range(count.bit_length() - 1)]


def first_columns(grid, own):
    x_home = lambda z: z // 2
    current = own
    steps = bits(grid.narrow)
    for place, bit in enumerate(reversed(steps)):

        def source(x, a, z):
            return (x ^ bit, a, z) if a == z % 2 else (x, 1 - a, z ^ 1)

        got = grid.send(current, source)
        if place < len(steps) - 1:
            rest = (grid.x ^ (grid.z // 2)) & (2 * bit - 1)
            current = jnp.where((rest == bit) & (grid.a == grid.z % 2), got, current)
        elif len(steps) > 1:
            rest = (grid.x ^ (grid.z // 2)) & (2 * bit - 1)
            got = jnp.where(rest == bit, got, current)
    return got


def load_first(narrow, refs, row_pts, col_pts):
    own, got, passed = refs
    x, a, z = (lax.axis_index(n) for n in ("narrow", "aux", "wide"))
    home = (x == z // 2) & (narrow == 2)
    core = a == z % 2
    row_pts[...] = own[...]

    @pl.when(home & core)
    def _():
        col_pts[...] = own[...]

    @pl.when(home != core)
    def _():
        col_pts[...] = got[...]

    @pl.when(jnp.logical_not(home | core))
    def _():
        col_pts[...] = passed[...]


def load_next(narrow, refs, row_pts, col_pts):
    kept, passed, first, second = refs
    x, a, z = (lax.axis_index(n) for n in ("narrow", "aux", "wide"))
    half = kept.shape[0]
    top = (z ^ (2 * x + a)) // narrow
    side = a ^ (1 - top)
    at = lambda which: pl.ds(pl.multiple_of(which * half, 8), half)
    col_pts[at(a), :] = kept[...]
    col_pts[at(1 - a), :] = passed[...]
    row_pts[at(side), :] = first[...]
    row_pts[at(1 - side), :] = second[...]


def shards(dissimilarity, config):
    grid = Grid()
    dims = config.shape[1]
    cols = dissimilarity.shape[1]
    scale = 1.0 / (cols * grid.wide)
    own = config.T
    got = first_columns(grid, own)
    got, norm = lax.optimization_barrier((got, norm_call(dissimilarity)))
    passed = grid.other_core(got)

    keep, send = tile_call(
        functools.partial(load_first, grid.narrow), scale, False, dims, dissimilarity, norm, own, got, passed
    )
    for iteration in range(1, ITERS):
        half = keep + grid.other_core(send)
        for bit in bits(grid.narrow):
            half = half + grid.across(half, "narrow", bit)
        first = grid.send(half, grid.spread(True))
        second = grid.send(half, grid.spread(False))
        other = grid.other_core(half)
        keep, send = tile_call(
            functools.partial(load_next, grid.narrow),
            scale, iteration + 1 == ITERS, dims, dissimilarity, norm, half, other, first, second
        )

    half = keep + grid.other_core(send)
    early = []
    if grid.wide == 4:
        sums = half[:SUMS, cols:]
        early = [grid.send(sums, lambda x, a, z: (x, a, z ^ 2)), grid.send(sums, lambda x, a, z: (x ^ 1, a, z ^ 2))]
    for bit in bits(grid.narrow):
        half = half + grid.across(half, "narrow", bit)
    sums = half[:SUMS, cols:]
    for part in early:
        sums = sums + part
    if not early:
        for bit in bits(grid.wide)[1:]:
            sums = sums + grid.across(sums, "wide", bit)
    half = half[:, :cols]
    first = grid.send(half, grid.spread(True))
    second = grid.send(half, grid.spread(False))
    stress = stress_call(sums, grid.across(sums, "wide", 1))
    first, second, stress = lax.optimization_barrier((first, second, stress))
    in_order = grid.spread_half() == 0
    embedding = jnp.where(
        in_order, jnp.concatenate([first, second], axis=0), jnp.concatenate([second, first], axis=0)
    )
    return embedding.T, stress


def solution(mesh):
    placed = (P(("groups", "narrow", "aux"), "wide"), P(("groups", "narrow", "aux"), None))
    return jax.shard_map(
        shards,
        mesh=mesh,
        in_specs=placed,
        out_specs=(P(("groups", "narrow", "aux"), None), P("groups")),
        check_vma=False,
    )
```

```python
import functools

import jax
import jax.numpy as jnp
from jax import lax
from jax.experimental import pallas as pl
from jax.experimental.pallas import tpu as pltpu
from jax.sharding import PartitionSpec as P

FLOOR = 3.0
TINY = 1e-30
DEPTH = 256
LANES = 128
EXTRA = 16
PIECE = 32
SUMS = 16

f32 = jnp.float32
bf16 = jnp.bfloat16
AXES = ("wide", "narrow", "aux")


def split2(values):
    high = values.astype(bf16)
    return high, (values - high.astype(f32)).astype(bf16)


def split3(values):
    high = values.astype(bf16)
    rest = values - high.astype(f32)
    middle = rest.astype(bf16)
    return high, middle, (rest - middle.astype(f32)).astype(bf16)


def norm_rows(points, first):
    count = points.shape[1]
    squares = jnp.sum(points * points, axis=0, keepdims=True)
    row = lax.broadcasted_iota(jnp.int32, (EXTRA, count), 0)
    ones = 3 if first else 0
    parts = 0 if first else 3
    rows = jnp.where((row >= ones) & (row < ones + 3), 1.0, 0.0)
    for k, part in enumerate(split3(squares)):
        rows = jnp.where(row == parts + k, part.astype(f32), rows)
    return rows.astype(bf16)


def tile_terms(row_pts, col_pts, delta_at, lhs, rhs, left, square, r_high, r_low, stress, emit):
    dims, rows = row_pts.shape
    cols = col_pts.shape[1]
    step = r_high.shape[2]
    points = row_pts[...]
    shift = jnp.sum(points, axis=1, keepdims=True) * (1.0 / rows)
    points = points - shift
    high, middle = split2(points)
    minus2 = lambda v: (v.astype(f32) * -2.0).astype(bf16)
    fill = DEPTH - 3 * dims - EXTRA
    lhs[...] = jnp.concatenate(
        [minus2(high), minus2(high), minus2(middle), norm_rows(points, True), jnp.zeros((fill, rows), bf16)], axis=0
    ).T
    left[...] = jnp.concatenate([high, middle, jnp.ones((EXTRA, rows), bf16)], axis=0)
    points = col_pts[...] - shift
    col_pts[...] = points
    high, middle = split2(points)
    rhs[...] = jnp.concatenate(
        [high, middle, high, norm_rows(points, False), jnp.zeros((fill, cols), bf16)], axis=0
    )

    def gram(c):
        square[c % 2] = jnp.dot(lhs[...], rhs[:, c * step:(c + 1) * step], preferred_element_type=f32)

    misfit = [jnp.zeros((16, step), f32)] * 2
    gram(0)
    for c in range(cols // step):
        if (c + 1) * step < cols:
            gram(c + 1)
        js = pl.ds(c * step, step)
        slot = c % 2
        for p in range(rows // PIECE):
            ps = pl.ds(p * PIECE, PIECE)
            squared = square[slot, ps, :]
            delta = delta_at(p * PIECE, js).astype(f32)
            above = c - p * PIECE // step
            if stress and above >= 0:
                inverse = lax.rsqrt(jnp.maximum(squared, TINY))
                ratio = delta * jnp.minimum(inverse, 1.0 / FLOOR)
                gap = delta - jnp.maximum(squared, 0.0) * inverse
                gap = gap * gap
                for q in range(0, PIECE, 16):
                    misfit[above > 0] = misfit[above > 0] + gap[q:q + 16]
            else:
                ratio = delta * lax.rsqrt(jnp.maximum(squared, FLOOR * FLOOR))
            high, low = split2(ratio)
            r_high[slot, ps, :] = high
            r_low[slot, ps, :] = low
        terms = jnp.dot(left[...], r_high[slot], preferred_element_type=f32)
        terms = terms + jnp.dot(left[...], r_low[slot], preferred_element_type=f32)
        cross = terms[:dims] + terms[dims:2 * dims]
        emit(js, col_pts[:, js] * terms[2 * dims:2 * dims + 1] - cross)
    return jnp.sum(misfit[0] + 2.0 * misfit[1]) if stress else None


def tile_scratch(dims, rows, cols):
    step = 256 if cols % 256 == 0 else 128
    return [
        pltpu.VMEM((dims, rows), f32),
        pltpu.VMEM((dims, cols), f32),
        pltpu.VMEM((rows, DEPTH), bf16),
        pltpu.VMEM((DEPTH, cols), bf16),
        pltpu.VMEM((2 * dims + EXTRA, rows), bf16),
        pltpu.VMEM((2, rows, step), f32),
        pltpu.VMEM((2, rows, step), bf16),
        pltpu.VMEM((2, rows, step), bf16),
    ]


def call(body, name, outs, scratch, cost, *arrays):
    vmem = pl.BlockSpec(memory_space=pltpu.VMEM)
    flops, size, roots = cost
    return pl.pallas_call(
        body,
        out_shape=[jax.ShapeDtypeStruct(shape, f32) for shape in outs],
        in_specs=[vmem] * len(arrays),
        out_specs=[vmem] * len(outs),
        scratch_shapes=scratch,
        compiler_params=pltpu.CompilerParams(vmem_limit_bytes=40 << 20),
        cost_estimate=pl.CostEstimate(flops=flops, bytes_accessed=size, transcendentals=roots),
        name=name,
    )(*arrays)


def tile_cost(rows, cols):
    return 2 * 3 * rows * cols * DEPTH, 2 * rows * cols, rows * cols


def first_tile(narrow, scale, delta, own, got, passed):
    dims, rows = own.shape
    cols = delta.shape[1]
    half = dims // 2

    def body(delta_ref, own_ref, got_ref, passed_ref, keep_ref, send_ref, result, row_pts, col_pts, *rest):
        x, a, z = (lax.axis_index(n) for n in ("narrow", "aux", "wide"))
        home = (x == z // 2) & (narrow == 2)
        core = a == z % 2
        row_pts[...] = own_ref[...]

        @pl.when(home & core)
        def _():
            col_pts[...] = own_ref[...]

        @pl.when(home != core)
        def _():
            col_pts[...] = got_ref[...]

        @pl.when(jnp.logical_not(home | core))
        def _():
            col_pts[...] = passed_ref[...]

        def emit(js, part):
            result[:, js] = part * scale

        tile_terms(row_pts, col_pts, lambda p, js: delta_ref[pl.ds(p, PIECE), js], *rest, False, emit)
        for ref, which in ((keep_ref, a), (send_ref, 1 - a)):
            ref[...] = result[pl.ds(pl.multiple_of(which * half, 8), half), :]

    scratch = [pltpu.VMEM((dims, cols), f32)] + tile_scratch(dims, rows, cols)
    outs = [(half, cols)] * 2
    return call(body, "tile_first", outs, scratch, tile_cost(rows, cols), delta, own, got, passed)


def next_tile(side_of, scale, delta, kept, passed, first, second, norm):
    half, rows = first.shape
    dims = 2 * half
    cols = delta.shape[1]

    def body(delta_ref, kept_ref, passed_ref, first_ref, second_ref, norm_ref, keep_ref, send_ref, result, *rest):
        row_pts, col_pts, *rest = rest
        a = lax.axis_index("aux")
        at = lambda which: pl.ds(pl.multiple_of(which * half, 8), half)
        side = side_of()
        col_pts[at(a), :] = kept_ref[...]
        col_pts[at(1 - a), :] = passed_ref[...]
        row_pts[at(side), :] = first_ref[...]
        row_pts[at(1 - side), :] = second_ref[...]

        def emit(js, part):
            result[:, js] = part * scale

        misfit = tile_terms(row_pts, col_pts, lambda p, js: delta_ref[pl.ds(p, PIECE), js], *rest, True, emit)
        for ref, which in ((keep_ref, a), (send_ref, 1 - a)):
            ref[:, :cols] = result[at(which), :]
            ref[:8, cols:] = jnp.full((8, LANES), misfit)
            ref[8:16, cols:] = norm_ref[...]
            ref[16:, cols:] = jnp.zeros((half - 16, LANES), f32)

    scratch = [pltpu.VMEM((dims, cols), f32)] + tile_scratch(dims, rows, cols)
    outs = [(half, cols + LANES)] * 2
    return call(body, "tile_next", outs, scratch, tile_cost(rows, cols), delta, kept, passed, first, second, norm)


def norm_body(delta_ref, out_ref):
    rows, cols = delta_ref.shape
    total = jnp.zeros((8, LANES), f32)
    for ic in range(rows // LANES):
        for jc in range(cols // LANES):
            part = delta_ref[ic * LANES:(ic + 1) * LANES, jc * LANES:(jc + 1) * LANES].astype(f32)
            total = total + jnp.sum((part * part).reshape(LANES // 8, 8, LANES), axis=0)
    out_ref[...] = jnp.full((8, LANES), jnp.sum(total))


def norm_call(delta):
    return call(norm_body, "norm", [(8, LANES)], [], (4 * delta.size, 2 * delta.size, 0), delta)[0]


class Grid:
    def __init__(self):
        self.narrow = lax.axis_size("narrow")
        self.wide = lax.axis_size("wide")
        assert lax.axis_size("aux") == 2 and self.wide == 2 * self.narrow

    def pairs(self, source):
        place = lambda x, a, z: (z * self.narrow + x) * 2 + a
        return [
            (place(*source(x, a, z)), place(x, a, z))
            for z in range(self.wide)
            for x in range(self.narrow)
            for a in range(2)
        ]

    def send(self, value, source):
        return lax.ppermute(value, AXES, self.pairs(source))

    def other_core(self, value):
        return lax.ppermute(value, "aux", [(0, 1), (1, 0)])

    def across(self, value, axis, bit):
        return lax.ppermute(value, axis, [(i, i ^ bit) for i in range(lax.axis_size(axis))])

    def spread(self, first):
        def source(x, a, z):
            block = 2 * x + a
            offset = z ^ block
            top, low = offset // self.narrow, offset % self.narrow
            if first:
                return x ^ low, a ^ (1 - top), block
            return x ^ low ^ (1 - top), a ^ top, block

        return source

    def spread_half(self):
        x, a, z = (lax.axis_index(n) for n in ("narrow", "aux", "wide"))
        return a ^ 1 ^ ((z ^ (2 * x + a)) >> (self.narrow.bit_length() - 1))


def bits(count):
    return [1 << k for k in range(count.bit_length() - 1)]


def first_columns(grid, own):
    x, a, z = (lax.axis_index(n) for n in ("narrow", "aux", "wide"))
    current = own
    steps = bits(grid.narrow)
    for place, bit in enumerate(reversed(steps)):

        def source(x, a, z):
            return (x ^ bit, a, z) if a == z % 2 else (x, 1 - a, z ^ 1)

        got = grid.send(current, source)
        if place < len(steps) - 1:
            rest = (x ^ (z // 2)) & (2 * bit - 1)
            current = jnp.where((rest == bit) & (a == z % 2), got, current)
        elif len(steps) > 1:
            rest = (x ^ (z // 2)) & (2 * bit - 1)
            got = jnp.where(rest == bit, got, current)
    return got


def shards(dissimilarity, config):
    grid = Grid()
    cols = dissimilarity.shape[1]
    scale = 1.0 / (cols * grid.wide)
    own = config.T
    got = first_columns(grid, own)
    got, norm = lax.optimization_barrier((got, norm_call(dissimilarity)))
    passed = grid.other_core(got)

    keep, send = first_tile(grid.narrow, scale, dissimilarity, own, got, passed)
    half = keep + grid.other_core(send)
    for bit in bits(grid.narrow):
        half = half + grid.across(half, "narrow", bit)
    first = grid.send(half, grid.spread(True))
    second = grid.send(half, grid.spread(False))
    other = grid.other_core(half)
    keep, send = next_tile(grid.spread_half, scale, dissimilarity, half, other, first, second, norm)

    half = keep + grid.other_core(send)
    early = []
    if grid.wide == 4:
        sums = half[:SUMS, cols:]
        early = [grid.send(sums, lambda x, a, z: (x, a, z ^ 2)), grid.send(sums, lambda x, a, z: (x ^ 1, a, z ^ 2))]
    for bit in bits(grid.narrow):
        half = half + grid.across(half, "narrow", bit)
    sums = half[:SUMS, cols:]
    if not early:
        for bit in bits(grid.wide)[1:]:
            sums = sums + grid.across(sums, "wide", bit)
    for part in early:
        sums = sums + part
    half = half[:, :cols]
    first = grid.send(half, grid.spread(True))
    second = grid.send(half, grid.spread(False))
    sums = sums + grid.across(sums, "wide", 1)
    first, second, sums = lax.optimization_barrier((first, second, sums))
    stress = lax.optimization_barrier(sums[:8] / sums[8:])[0, :1]
    in_order = grid.spread_half() == 0
    embedding = jnp.where(
        in_order, jnp.concatenate([first, second], axis=0), jnp.concatenate([second, first], axis=0)
    )
    return embedding.T, stress


def solution(mesh):
    placed = (P(("groups", "narrow", "aux"), "wide"), P(("groups", "narrow", "aux"), None))
    return jax.shard_map(
        shards,
        mesh=mesh,
        in_specs=placed,
        out_specs=(P(("groups", "narrow", "aux"), None), P("groups")),
        check_vma=False,
    )
```

```python
import functools

import jax
import jax.numpy as jnp
from jax import lax
from jax.experimental import pallas as pl
from jax.experimental.pallas import tpu as pltpu
from jax.sharding import PartitionSpec as P

FLOOR = 3.0
TINY = 1e-30
DEPTH = 256
LANES = 128
EXTRA = 16
PIECE = 32
SUMS = 16

f32 = jnp.float32
bf16 = jnp.bfloat16
AXES = ("wide", "narrow", "aux")


def split2(values):
    high = values.astype(bf16)
    return high, (values - high.astype(f32)).astype(bf16)


def split3(values):
    high = values.astype(bf16)
    rest = values - high.astype(f32)
    middle = rest.astype(bf16)
    return high, middle, (rest - middle.astype(f32)).astype(bf16)


def norm_rows(points, first):
    count = points.shape[1]
    squares = jnp.sum(points * points, axis=0, keepdims=True)
    row = lax.broadcasted_iota(jnp.int32, (EXTRA, count), 0)
    ones = 3 if first else 0
    parts = 0 if first else 3
    rows = jnp.where((row >= ones) & (row < ones + 3), 1.0, 0.0)
    for k, part in enumerate(split3(squares)):
        rows = jnp.where(row == parts + k, part.astype(f32), rows)
    return rows.astype(bf16)


def tile_terms(row_pts, col_pts, delta_at, lhs, rhs, left, square, r_high, r_low, stress, emit):
    dims, rows = row_pts.shape
    cols = col_pts.shape[1]
    step = r_high.shape[2]
    points = row_pts[...]
    shift = jnp.sum(points, axis=1, keepdims=True) * (1.0 / rows)
    points = points - shift
    high, middle = split2(points)
    minus2 = lambda v: (v.astype(f32) * -2.0).astype(bf16)
    fill = DEPTH - 3 * dims - EXTRA
    lhs[...] = jnp.concatenate(
        [minus2(high), minus2(high), minus2(middle), norm_rows(points, True), jnp.zeros((fill, rows), bf16)], axis=0
    ).T
    lft = jnp.concatenate([high, middle, jnp.ones((EXTRA, rows), bf16)], axis=0)
    left[:, :rows] = lft
    left[:, rows:] = lft
    points = col_pts[...] - shift
    col_pts[...] = points
    high, middle = split2(points)
    rhs[...] = jnp.concatenate(
        [high, middle, high, norm_rows(points, False), jnp.zeros((fill, cols), bf16)], axis=0
    )

    def gram(c):
        square[c % 2] = jnp.dot(lhs[...], rhs[:, c * step:(c + 1) * step], preferred_element_type=f32)

    misfit = [jnp.zeros((16, step), f32)] * 2
    gram(0)
    for c in range(cols // step):
        if (c + 1) * step < cols:
            gram(c + 1)
        js = pl.ds(c * step, step)
        slot = c % 2
        for p in range(rows // PIECE):
            ps = pl.ds(p * PIECE, PIECE)
            squared = square[slot, ps, :]
            delta = delta_at(p * PIECE, js).astype(f32)
            above = c - p * PIECE // step
            if stress and above >= 0:
                inverse = lax.rsqrt(jnp.maximum(squared, TINY))
                ratio = delta * jnp.minimum(inverse, 1.0 / FLOOR)
                gap = delta - jnp.maximum(squared, 0.0) * inverse
                gap = gap * gap
                for q in range(0, PIECE, 16):
                    misfit[above > 0] = misfit[above > 0] + gap[q:q + 16]
            else:
                ratio = delta * lax.rsqrt(jnp.maximum(squared, FLOOR * FLOOR))
            high, low = split2(ratio)
            r_high[slot, ps, :] = high
            r_high[slot, pl.ds(rows + p * PIECE, PIECE), :] = low
        terms = jnp.dot(left[...], r_high[slot], preferred_element_type=f32)
        cross = terms[:dims] + terms[dims:2 * dims]
        emit(js, col_pts[:, js] * terms[2 * dims:2 * dims + 1] - cross)
    return jnp.sum(misfit[0] + 2.0 * misfit[1]) if stress else None


def tile_scratch(dims, rows, cols):
    step = 256 if cols % 256 == 0 else 128
    return [
        pltpu.VMEM((dims, rows), f32),
        pltpu.VMEM((dims, cols), f32),
        pltpu.VMEM((rows, DEPTH), bf16),
        pltpu.VMEM((DEPTH, cols), bf16),
        pltpu.VMEM((2 * dims + EXTRA, 2 * rows), bf16),
        pltpu.VMEM((2, rows, step), f32),
        pltpu.VMEM((2, 2 * rows, step), bf16),
        pltpu.VMEM((8, LANES), bf16),
    ]


def call(body, name, outs, scratch, cost, *arrays):
    vmem = pl.BlockSpec(memory_space=pltpu.VMEM)
    flops, size, roots = cost
    return pl.pallas_call(
        body,
        out_shape=[jax.ShapeDtypeStruct(shape, f32) for shape in outs],
        in_specs=[vmem] * len(arrays),
        out_specs=[vmem] * len(outs),
        scratch_shapes=scratch,
        compiler_params=pltpu.CompilerParams(vmem_limit_bytes=40 << 20),
        cost_estimate=pl.CostEstimate(flops=flops, bytes_accessed=size, transcendentals=roots),
        name=name,
    )(*arrays)


def tile_cost(rows, cols):
    return 2 * 3 * rows * cols * DEPTH, 2 * rows * cols, rows * cols


def first_tile(narrow, scale, delta, own, got, passed):
    dims, rows = own.shape
    cols = delta.shape[1]
    half = dims // 2

    def body(delta_ref, own_ref, got_ref, passed_ref, keep_ref, send_ref, result, row_pts, col_pts, *rest):
        x, a, z = (lax.axis_index(n) for n in ("narrow", "aux", "wide"))
        home = (x == z // 2) & (narrow == 2)
        core = a == z % 2
        row_pts[...] = own_ref[...]

        @pl.when(home & core)
        def _():
            col_pts[...] = own_ref[...]

        @pl.when(home != core)
        def _():
            col_pts[...] = got_ref[...]

        @pl.when(jnp.logical_not(home | core))
        def _():
            col_pts[...] = passed_ref[...]

        def emit(js, part):
            result[:, js] = part * scale

        tile_terms(row_pts, col_pts, lambda p, js: delta_ref[pl.ds(p, PIECE), js], *rest, False, emit)
        for ref, which in ((keep_ref, a), (send_ref, 1 - a)):
            ref[...] = result[pl.ds(pl.multiple_of(which * half, 8), half), :]

    scratch = [pltpu.VMEM((dims, cols), f32)] + tile_scratch(dims, rows, cols)
    outs = [(half, cols)] * 2
    return call(body, "tile_first", outs, scratch, tile_cost(rows, cols), delta, own, got, passed)


def next_tile(side_of, scale, delta, kept, passed, first, second, norm):
    half, rows = first.shape
    dims = 2 * half
    cols = delta.shape[1]

    def body(delta_ref, kept_ref, passed_ref, first_ref, second_ref, norm_ref, keep_ref, send_ref, result, *rest):
        row_pts, col_pts, *rest = rest
        a = lax.axis_index("aux")
        at = lambda which: pl.ds(pl.multiple_of(which * half, 8), half)
        side = side_of()
        col_pts[at(a), :] = kept_ref[...]
        col_pts[at(1 - a), :] = passed_ref[...]
        row_pts[at(side), :] = first_ref[...]
        row_pts[at(1 - side), :] = second_ref[...]

        def emit(js, part):
            result[:, js] = part * scale

        misfit = tile_terms(row_pts, col_pts, lambda p, js: delta_ref[pl.ds(p, PIECE), js], *rest, True, emit)
        for ref, which in ((keep_ref, a), (send_ref, 1 - a)):
            ref[:, :cols] = result[at(which), :]
            ref[:8, cols:] = jnp.full((8, LANES), misfit)
            ref[8:16, cols:] = norm_ref[...]
            ref[16:, cols:] = jnp.zeros((half - 16, LANES), f32)

    scratch = [pltpu.VMEM((dims, cols), f32)] + tile_scratch(dims, rows, cols)
    outs = [(half, cols + LANES)] * 2
    return call(body, "tile_next", outs, scratch, tile_cost(rows, cols), delta, kept, passed, first, second, norm)


def norm_body(delta_ref, out_ref):
    rows, cols = delta_ref.shape
    total = jnp.zeros((8, LANES), f32)
    for ic in range(rows // LANES):
        for jc in range(cols // LANES):
            part = delta_ref[ic * LANES:(ic + 1) * LANES, jc * LANES:(jc + 1) * LANES].astype(f32)
            total = total + jnp.sum((part * part).reshape(LANES // 8, 8, LANES), axis=0)
    out_ref[...] = jnp.full((8, LANES), jnp.sum(total))


def norm_call(delta):
    return call(norm_body, "norm", [(8, LANES)], [], (4 * delta.size, 2 * delta.size, 0), delta)[0]


def stress_body(mine_ref, other_ref, out_ref):
    total = mine_ref[...] + other_ref[...]
    out_ref[0] = (total[:8] / total[8:])[0, 0]


def stress_call(mine, other):
    vmem = pl.BlockSpec(memory_space=pltpu.VMEM)
    return pl.pallas_call(
        stress_body,
        out_shape=jax.ShapeDtypeStruct((1,), f32),
        in_specs=[vmem] * 2,
        out_specs=pl.BlockSpec(memory_space=pltpu.SMEM),
        compiler_params=pltpu.CompilerParams(vmem_limit_bytes=40 << 20),
        name="stress",
    )(mine, other)


class Grid:
    def __init__(self):
        self.narrow = lax.axis_size("narrow")
        self.wide = lax.axis_size("wide")
        assert lax.axis_size("aux") == 2 and self.wide == 2 * self.narrow

    def pairs(self, source):
        place = lambda x, a, z: (z * self.narrow + x) * 2 + a
        return [
            (place(*source(x, a, z)), place(x, a, z))
            for z in range(self.wide)
            for x in range(self.narrow)
            for a in range(2)
        ]

    def send(self, value, source):
        return lax.ppermute(value, AXES, self.pairs(source))

    def other_core(self, value):
        return lax.ppermute(value, "aux", [(0, 1), (1, 0)])

    def across(self, value, axis, bit):
        return lax.ppermute(value, axis, [(i, i ^ bit) for i in range(lax.axis_size(axis))])

    def spread(self, late, flip=0):
        def source(x, a, z):
            block = 2 * x + a
            offset = z ^ block
            top, low = offset // self.narrow, offset % self.narrow
            if late:
                return x ^ low ^ (1 - top), a ^ top, block
            return x ^ low ^ flip, a ^ (1 - top), block

        return source

    def early(self, value):
        return self.send(value, self.spread(False)), self.send(value, self.spread(False, 1))

    def spread_half(self):
        x, a, z = (lax.axis_index(n) for n in ("narrow", "aux", "wide"))
        return a ^ 1 ^ ((z ^ (2 * x + a)) >> (self.narrow.bit_length() - 1))


def bits(count):
    return [1 << k for k in range(count.bit_length() - 1)]


def first_columns(grid, own):
    x, a, z = (lax.axis_index(n) for n in ("narrow", "aux", "wide"))
    current = own
    steps = bits(grid.narrow)
    for place, bit in enumerate(reversed(steps)):

        def source(x, a, z):
            return (x ^ bit, a, z) if a == z % 2 else (x, 1 - a, z ^ 1)

        got = grid.send(current, source)
        if place < len(steps) - 1:
            rest = (x ^ (z // 2)) & (2 * bit - 1)
            current = jnp.where((rest == bit) & (a == z % 2), got, current)
        elif len(steps) > 1:
            rest = (x ^ (z // 2)) & (2 * bit - 1)
            got = jnp.where(rest == bit, got, current)
    return got


def shards(dissimilarity, config):
    grid = Grid()
    cols = dissimilarity.shape[1]
    scale = 1.0 / (cols * grid.wide)
    own = config.T
    got = first_columns(grid, own)
    got, norm = lax.optimization_barrier((got, norm_call(dissimilarity)))
    passed = grid.other_core(got)

    keep, send = first_tile(grid.narrow, scale, dissimilarity, own, got, passed)
    half = keep + grid.other_core(send)
    for bit in bits(grid.narrow)[1:]:
        half = half + grid.across(half, "narrow", bit)
    first = grid.early(half)
    half = half + grid.across(half, "narrow", 1)
    first = first[0] + first[1]
    second = grid.send(half, grid.spread(True))
    other = grid.other_core(half)
    keep, send = next_tile(grid.spread_half, scale, dissimilarity, half, other, first, second, norm)

    half = keep + grid.other_core(send)
    early = []
    if grid.wide == 4:
        sums = half[:SUMS, cols:]
        early = [grid.send(sums, lambda x, a, z: (x, a, z ^ 2)), grid.send(sums, lambda x, a, z: (x ^ 1, a, z ^ 2))]
    for bit in bits(grid.narrow):
        half = half + grid.across(half, "narrow", bit)
    sums = half[:SUMS, cols:]
    if not early:
        for bit in bits(grid.wide)[1:]:
            sums = sums + grid.across(sums, "wide", bit)
    for part in early:
        sums = sums + part
    half = half[:, :cols]
    first = grid.send(half, grid.spread(False))
    second = grid.send(half, grid.spread(True))
    stress = stress_call(sums, grid.across(sums, "wide", 1))
    first, second, stress = lax.optimization_barrier((first, second, stress))
    in_order = grid.spread_half() == 0
    embedding = jnp.where(
        in_order, jnp.concatenate([first, second], axis=0), jnp.concatenate([second, first], axis=0)
    )
    return embedding.T, stress


def solution(mesh):
    placed = (P(("groups", "narrow", "aux"), "wide"), P(("groups", "narrow", "aux"), None))
    return jax.shard_map(
        shards,
        mesh=mesh,
        in_specs=placed,
        out_specs=(P(("groups", "narrow", "aux"), None), P("groups")),
        check_vma=False,
    )
```

```python
import functools

import jax
import jax.numpy as jnp
from jax import lax
from jax.experimental import pallas as pl
from jax.experimental.pallas import tpu as pltpu
from jax.sharding import PartitionSpec as P

FLOOR = 3.0
TINY = 1e-30
DEPTH = 256
LANES = 128
EXTRA = 16
PIECE = 32
TILE_SCRATCH = 8
SUMS = 16

f32 = jnp.float32
bf16 = jnp.bfloat16
AXES = ("wide", "narrow", "aux")


def split2(values):
    high = values.astype(bf16)
    return high, (values - high.astype(f32)).astype(bf16)


def split3(values):
    high = values.astype(bf16)
    rest = values - high.astype(f32)
    middle = rest.astype(bf16)
    return high, middle, (rest - middle.astype(f32)).astype(bf16)


def norm_rows(points, first):
    count = points.shape[1]
    squares = jnp.sum(points * points, axis=0, keepdims=True)
    row = lax.broadcasted_iota(jnp.int32, (EXTRA, count), 0)
    ones = 3 if first else 0
    parts = 0 if first else 3
    rows = jnp.where((row >= ones) & (row < ones + 3), 1.0, 0.0)
    for k, part in enumerate(split3(squares)):
        rows = jnp.where(row == parts + k, part.astype(f32), rows)
    return rows.astype(bf16)


def tile_terms(row_pts, col_pts, delta_at, lhs, rhs, left, square, r_high, r_low, stress, emit):
    dims, rows = row_pts.shape
    cols = col_pts.shape[1]
    step = r_high.shape[2]
    points = row_pts[...]
    shift = jnp.sum(points, axis=1, keepdims=True) * (1.0 / rows)
    points = points - shift
    high, middle = split2(points)
    minus2 = lambda v: (v.astype(f32) * -2.0).astype(bf16)
    fill = DEPTH - 3 * dims - EXTRA
    lhs[...] = jnp.concatenate(
        [minus2(high), minus2(high), minus2(middle), norm_rows(points, True), jnp.zeros((fill, rows), bf16)], axis=0
    ).T
    lft = jnp.concatenate([high, middle, jnp.ones((EXTRA, rows), bf16)], axis=0)
    left[:, :rows] = lft
    left[:, rows:] = lft
    points = col_pts[...] - shift
    col_pts[...] = points
    high, middle = split2(points)
    rhs[...] = jnp.concatenate(
        [high, middle, high, norm_rows(points, False), jnp.zeros((fill, cols), bf16)], axis=0
    )

    def gram(c):
        square[c % 2] = jnp.dot(lhs[...], rhs[:, c * step:(c + 1) * step], preferred_element_type=f32)

    misfit = jnp.zeros((16, step), f32)
    gram(0)
    for c in range(cols // step):
        if (c + 1) * step < cols:
            gram(c + 1)
        js = pl.ds(c * step, step)
        slot = c % 2
        for p in range(rows // PIECE):
            ps = pl.ds(p * PIECE, PIECE)
            squared = square[slot, ps, :]
            delta = delta_at(p * PIECE, js).astype(f32)
            if stress:
                inverse = lax.rsqrt(jnp.maximum(squared, TINY))
                ratio = delta * jnp.minimum(inverse, 1.0 / FLOOR)
                gap = delta - jnp.maximum(squared, 0.0) * inverse
                gap = gap * gap
                for q in range(0, PIECE, 16):
                    misfit = misfit + gap[q:q + 16]
            else:
                ratio = delta * lax.rsqrt(jnp.maximum(squared, FLOOR * FLOOR))
            high, low = split2(ratio)
            r_high[slot, ps, :] = high
            r_high[slot, pl.ds(rows + p * PIECE, PIECE), :] = low
        terms = jnp.dot(left[...], r_high[slot], preferred_element_type=f32)
        cross = terms[:dims] + terms[dims:2 * dims]
        emit(js, col_pts[:, js] * terms[2 * dims:2 * dims + 1] - cross)
    return jnp.sum(misfit) if stress else None


def tile_scratch(dims, rows, cols):
    step = 256 if cols % 256 == 0 else 128
    return [
        pltpu.VMEM((dims, rows), f32),
        pltpu.VMEM((dims, cols), f32),
        pltpu.VMEM((rows, DEPTH), bf16),
        pltpu.VMEM((DEPTH, cols), bf16),
        pltpu.VMEM((2 * dims + EXTRA, 2 * rows), bf16),
        pltpu.VMEM((2, rows, step), f32),
        pltpu.VMEM((2, 2 * rows, step), bf16),
        pltpu.VMEM((8, LANES), bf16),
    ]


def call(body, name, outs, scratch, cost, *arrays):
    vmem = pl.BlockSpec(memory_space=pltpu.VMEM)
    flops, size, roots = cost
    return pl.pallas_call(
        body,
        out_shape=[jax.ShapeDtypeStruct(shape, f32) for shape in outs],
        in_specs=[vmem] * len(arrays),
        out_specs=[vmem] * len(outs),
        scratch_shapes=scratch,
        compiler_params=pltpu.CompilerParams(vmem_limit_bytes=40 << 20),
        cost_estimate=pl.CostEstimate(flops=flops, bytes_accessed=size, transcendentals=roots),
        name=name,
    )(*arrays)


def tile_cost(rows, cols):
    return 2 * 3 * rows * cols * DEPTH, 2 * rows * cols, rows * cols


def first_tile(narrow, scale, delta, own, got, passed):
    dims, rows = own.shape
    cols = delta.shape[1]
    half = cols // 2

    def body(delta_ref, own_ref, got_ref, passed_ref, keep_ref, send_ref, result, row_pts, col_pts, *rest):
        x, a, z = (lax.axis_index(n) for n in ("narrow", "aux", "wide"))
        home = (x == z // 2) & (narrow == 2)
        core = a == z % 2
        row_pts[...] = own_ref[...]

        @pl.when(home & core)
        def _():
            col_pts[...] = own_ref[...]

        @pl.when(home != core)
        def _():
            col_pts[...] = got_ref[...]

        @pl.when(jnp.logical_not(home | core))
        def _():
            col_pts[...] = passed_ref[...]

        def emit(js, part):
            result[:, js] = part * scale

        tile_terms(row_pts, col_pts, lambda p, js: delta_ref[pl.ds(p, PIECE), js], *rest, False, emit)
        for ref, which in ((keep_ref, a), (send_ref, 1 - a)):
            ref[...] = result[:, pl.ds(pl.multiple_of(which * half, LANES), half)]

    scratch = [pltpu.VMEM((dims, cols), f32)] + tile_scratch(dims, rows, cols)
    outs = [(dims, half)] * 2
    return call(body, "tile_first", outs, scratch, tile_cost(rows, cols), delta, own, got, passed)


def next_tile(side_of, scale, delta, rows_in, kept, passed, norm, before=None):
    dims, rows = rows_in.shape
    cols = delta.shape[1]
    half, less = cols // 2, dims // 2
    closing = before is not None

    def body(delta_ref, rows_ref, kept_ref, passed_ref, sums_ref, *refs):
        row_pts, col_pts, *rest = refs[-TILE_SCRATCH:]
        refs = refs[:-TILE_SCRATCH]
        a = lax.axis_index("aux")
        at = lambda which: pl.ds(pl.multiple_of(which * half, LANES), half)
        base = side_of() * rows
        row_pts[...] = rows_ref[...]
        col_pts[:, at(a)] = kept_ref[...]
        col_pts[:, at(1 - a)] = passed_ref[...]

        def delta_at(p, js):
            return delta_ref[pl.ds(pl.multiple_of(base + p, PIECE), PIECE), js]

        if not closing:
            part_ref, out_sums_ref = refs

            def emit(js, part):
                part_ref[:, js] = part

            misfit = tile_terms(row_pts, col_pts, delta_at, *rest, True, emit)
            out_sums_ref[:8] = jnp.full((8, LANES), misfit)
            out_sums_ref[8:] = sums_ref[...]
            return
        before_ref, keep_ref, send_ref, result = refs

        def emit(js, part):
            result[:, js] = (before_ref[:, js] + part) * scale

        misfit = tile_terms(row_pts, col_pts, delta_at, *rest, True, emit)
        for ref, which in ((keep_ref, a), (send_ref, 1 - a)):
            ref[:, :cols] = result[pl.ds(pl.multiple_of(which * less, 8), less), :]
            ref[:8, cols:] = sums_ref[:8] + misfit
            ref[8:16, cols:] = sums_ref[8:]
            ref[16:, cols:] = jnp.zeros((less - 16, LANES), f32)

    scratch = tile_scratch(dims, rows, cols)
    cost = tile_cost(rows, cols)
    if not closing:
        outs = [(dims, cols), (SUMS, LANES)]
        return call(body, "tile_open", outs, scratch, cost, delta, rows_in, kept, passed, norm)
    scratch = [pltpu.VMEM((dims, cols), f32)] + scratch
    outs = [(less, cols + LANES)] * 2
    return call(body, "tile_close", outs, scratch, cost, delta, rows_in, kept, passed, norm, before)


def norm_body(delta_ref, out_ref):
    rows, cols = delta_ref.shape
    total = jnp.zeros((8, LANES), f32)
    for ic in range(rows // LANES):
        for jc in range(cols // LANES):
            part = delta_ref[ic * LANES:(ic + 1) * LANES, jc * LANES:(jc + 1) * LANES].astype(f32)
            total = total + jnp.sum((part * part).reshape(LANES // 8, 8, LANES), axis=0)
    out_ref[...] = jnp.full((8, LANES), jnp.sum(total))


def norm_call(delta):
    return call(norm_body, "norm", [(8, LANES)], [], (4 * delta.size, 2 * delta.size, 0), delta)[0]


def stress_body(mine_ref, other_ref, out_ref):
    total = mine_ref[...] + other_ref[...]
    out_ref[0] = (total[:8] / total[8:])[0, 0]


def stress_call(mine, other):
    vmem = pl.BlockSpec(memory_space=pltpu.VMEM)
    return pl.pallas_call(
        stress_body,
        out_shape=jax.ShapeDtypeStruct((1,), f32),
        in_specs=[vmem] * 2,
        out_specs=pl.BlockSpec(memory_space=pltpu.SMEM),
        compiler_params=pltpu.CompilerParams(vmem_limit_bytes=40 << 20),
        name="stress",
    )(mine, other)


class Grid:
    def __init__(self):
        self.narrow = lax.axis_size("narrow")
        self.wide = lax.axis_size("wide")
        assert lax.axis_size("aux") == 2 and self.wide == 2 * self.narrow

    def pairs(self, source):
        place = lambda x, a, z: (z * self.narrow + x) * 2 + a
        return [
            (place(*source(x, a, z)), place(x, a, z))
            for z in range(self.wide)
            for x in range(self.narrow)
            for a in range(2)
        ]

    def send(self, value, source):
        return lax.ppermute(value, AXES, self.pairs(source))

    def other_core(self, value):
        return lax.ppermute(value, "aux", [(0, 1), (1, 0)])

    def across(self, value, axis, bit):
        return lax.ppermute(value, axis, [(i, i ^ bit) for i in range(lax.axis_size(axis))])

    def spread(self, late, flip=0):
        def source(x, a, z):
            block = 2 * x + a
            offset = z ^ block
            top, low = offset // self.narrow, offset % self.narrow
            if late:
                return x ^ low ^ (1 - top), a ^ top, block
            return x ^ low ^ flip, a ^ (1 - top), block

        return source

    def early(self, value):
        return self.send(value, self.spread(False)), self.send(value, self.spread(False, 1))

    def spread_half(self):
        x, a, z = (lax.axis_index(n) for n in ("narrow", "aux", "wide"))
        return a ^ 1 ^ ((z ^ (2 * x + a)) >> (self.narrow.bit_length() - 1))


def bits(count):
    return [1 << k for k in range(count.bit_length() - 1)]


def first_columns(grid, own):
    x, a, z = (lax.axis_index(n) for n in ("narrow", "aux", "wide"))
    current = own
    steps = bits(grid.narrow)
    for place, bit in enumerate(reversed(steps)):

        def source(x, a, z):
            return (x ^ bit, a, z) if a == z % 2 else (x, 1 - a, z ^ 1)

        got = grid.send(current, source)
        if place < len(steps) - 1:
            rest = (x ^ (z // 2)) & (2 * bit - 1)
            current = jnp.where((rest == bit) & (a == z % 2), got, current)
        elif len(steps) > 1:
            rest = (x ^ (z // 2)) & (2 * bit - 1)
            got = jnp.where(rest == bit, got, current)
    return got


def shards(dissimilarity, config):
    grid = Grid()
    cols = dissimilarity.shape[1]
    scale = 1.0 / (cols * grid.wide)
    own = config.T
    got = first_columns(grid, own)
    got, norm = lax.optimization_barrier((got, norm_call(dissimilarity)))
    passed = grid.other_core(got)

    keep, send = first_tile(grid.narrow, scale, dissimilarity, own, got, passed)
    half = keep + grid.other_core(send)
    for bit in bits(grid.narrow)[1:]:
        half = half + grid.across(half, "narrow", bit)
    first = grid.early(half)
    half = half + grid.across(half, "narrow", 1)
    first = first[0] + first[1]
    second = grid.send(half, grid.spread(True))
    other = grid.other_core(half)
    part, sums = next_tile(grid.spread_half, scale, dissimilarity, first, half, other, norm)
    keep, send = next_tile(lambda: 1 - grid.spread_half(), scale, dissimilarity, second, half, other, sums, part)

    half = keep + grid.other_core(send)
    early = []
    if grid.wide == 4:
        sums = half[:SUMS, cols:]
        early = [grid.send(sums, lambda x, a, z: (x, a, z ^ 2)), grid.send(sums, lambda x, a, z: (x ^ 1, a, z ^ 2))]
    for bit in bits(grid.narrow):
        half = half + grid.across(half, "narrow", bit)
    sums = half[:SUMS, cols:]
    if not early:
        for bit in bits(grid.wide)[1:]:
            sums = sums + grid.across(sums, "wide", bit)
    for part in early:
        sums = sums + part
    half = half[:, :cols]
    first = grid.send(half, grid.spread(False))
    second = grid.send(half, grid.spread(True))
    stress = stress_call(sums, grid.across(sums, "wide", 1))
    first, second, stress = lax.optimization_barrier((first, second, stress))
    in_order = grid.spread_half() == 0
    embedding = jnp.where(
        in_order, jnp.concatenate([first, second], axis=0), jnp.concatenate([second, first], axis=0)
    )
    return embedding.T, stress


def solution(mesh):
    placed = (P(("groups", "narrow", "aux"), "wide"), P(("groups", "narrow", "aux"), None))
    return jax.shard_map(
        shards,
        mesh=mesh,
        in_specs=placed,
        out_specs=(P(("groups", "narrow", "aux"), None), P("groups")),
        check_vma=False,
    )
```

```python
import functools

import jax
import jax.numpy as jnp
from jax import lax
from jax.experimental import pallas as pl
from jax.experimental.pallas import tpu as pltpu
from jax.sharding import PartitionSpec as P

FLOOR = 3.0
TINY = 1e-30
DEPTH = 256
LANES = 128
EXTRA = 16
PIECE = 32
SUMS = 16

f32 = jnp.float32
bf16 = jnp.bfloat16
AXES = ("wide", "narrow", "aux")


def split2(values):
    high = values.astype(bf16)
    return high, (values - high.astype(f32)).astype(bf16)


def split3(values):
    high = values.astype(bf16)
    rest = values - high.astype(f32)
    middle = rest.astype(bf16)
    return high, middle, (rest - middle.astype(f32)).astype(bf16)


def norm_rows(points, first):
    count = points.shape[1]
    squares = jnp.sum(points * points, axis=0, keepdims=True)
    row = lax.broadcasted_iota(jnp.int32, (EXTRA, count), 0)
    ones = 3 if first else 0
    parts = 0 if first else 3
    rows = jnp.where((row >= ones) & (row < ones + 3), 1.0, 0.0)
    for k, part in enumerate(split3(squares)):
        rows = jnp.where(row == parts + k, part.astype(f32), rows)
    return rows.astype(bf16)


def tile_terms(row_pts, col_pts, delta_at, lhs, rhs, left, square, r_both, stress, emit):
    dims, rows = row_pts.shape
    cols = col_pts.shape[1]
    step = r_both.shape[2]
    points = row_pts[...]
    shift = jnp.sum(points, axis=1, keepdims=True) * (1.0 / rows)
    points = points - shift
    high, middle = split2(points)
    minus2 = lambda v: (v.astype(f32) * -2.0).astype(bf16)
    fill = DEPTH - 3 * dims - EXTRA
    lhs[...] = jnp.concatenate(
        [minus2(high), minus2(high), minus2(middle), norm_rows(points, True), jnp.zeros((fill, rows), bf16)], axis=0
    ).T
    factors = jnp.concatenate([high, middle, jnp.ones((EXTRA, rows), bf16)], axis=0)
    tall = r_both.shape[1] // 2
    for row in range(0, rows, tall):
        left[:, 2 * row:2 * row + tall] = factors[:, row:row + tall]
        left[:, 2 * row + tall:2 * (row + tall)] = factors[:, row:row + tall]
    points = col_pts[...] - shift
    col_pts[...] = points
    high, middle = split2(points)
    rhs[...] = jnp.concatenate(
        [high, middle, high, norm_rows(points, False), jnp.zeros((fill, cols), bf16)], axis=0
    )

    units = [(row, col) for col in range(0, cols, step) for row in range(0, rows, tall)]

    def gram(u):
        row, col = units[u]
        square[u % 2] = jnp.dot(lhs[row:row + tall, :], rhs[:, col:col + step], preferred_element_type=f32)

    misfit = jnp.zeros((16, step), f32)
    terms = None
    gram(0)
    for u, (row, col) in enumerate(units):
        if u + 1 < len(units):
            gram(u + 1)
        slot = u % 2
        for p in range(0, tall, PIECE):
            squared = square[slot, p:p + PIECE, :]
            delta = delta_at(row + p, col, step).astype(f32)
            if stress:
                inverse = lax.rsqrt(jnp.maximum(squared, TINY))
                ratio = delta * jnp.minimum(inverse, 1.0 / FLOOR)
                gap = delta - jnp.maximum(squared, 0.0) * inverse
                gap = gap * gap
                for q in range(0, PIECE, 16):
                    misfit = misfit + gap[q:q + 16]
            else:
                ratio = delta * lax.rsqrt(jnp.maximum(squared, FLOOR * FLOOR))
            high, low = split2(ratio)
            r_both[slot, p:p + PIECE, :] = high
            r_both[slot, tall + p:tall + p + PIECE, :] = low
        part = jnp.dot(left[:, 2 * row:2 * (row + tall)], r_both[slot], preferred_element_type=f32)
        terms = part if terms is None else terms + part
        if row + tall == rows:
            cross = terms[:dims] + terms[dims:2 * dims]
            js = pl.ds(col, step)
            emit(js, col_pts[:, js] * terms[2 * dims:2 * dims + 1] - cross)
            terms = None
    return jnp.sum(misfit) if stress else None


def tile_scratch(dims, rows, cols, tall=None, step=None):
    tall = tall or rows
    step = step or (256 if cols % 256 == 0 else LANES)
    return [
        pltpu.VMEM((dims, rows), f32),
        pltpu.VMEM((dims, cols), f32),
        pltpu.VMEM((rows, DEPTH), bf16),
        pltpu.VMEM((DEPTH, cols), bf16),
        pltpu.VMEM((2 * dims + EXTRA, 2 * rows), bf16),
        pltpu.VMEM((2, tall, step), f32),
        pltpu.VMEM((2, 2 * tall, step), bf16),
    ]


def call(body, name, outs, scratch, cost, *arrays):
    vmem = pl.BlockSpec(memory_space=pltpu.VMEM)
    flops, size, roots = cost
    return pl.pallas_call(
        body,
        out_shape=[jax.ShapeDtypeStruct(shape, f32) for shape in outs],
        in_specs=[vmem] * len(arrays),
        out_specs=[vmem] * len(outs),
        scratch_shapes=scratch,
        compiler_params=pltpu.CompilerParams(vmem_limit_bytes=40 << 20),
        cost_estimate=pl.CostEstimate(flops=flops, bytes_accessed=size, transcendentals=roots),
        name=name,
    )(*arrays)


def tile_cost(rows, cols):
    return 2 * 3 * rows * cols * DEPTH, 2 * rows * cols, rows * cols


def first_tile(narrow, scale, delta, own, got, passed):
    dims, rows = own.shape
    cols = delta.shape[1]
    half = cols // 2

    def body(delta_ref, own_ref, got_ref, passed_ref, keep_ref, send_ref, result, row_pts, col_pts, *rest):
        x, a, z = (lax.axis_index(n) for n in ("narrow", "aux", "wide"))
        home = (x == z // 2) & (narrow == 2)
        core = a == z % 2
        row_pts[...] = own_ref[...]

        @pl.when(home & core)
        def _():
            col_pts[...] = own_ref[...]

        @pl.when(home != core)
        def _():
            col_pts[...] = got_ref[...]

        @pl.when(jnp.logical_not(home | core))
        def _():
            col_pts[...] = passed_ref[...]

        def emit(js, part):
            result[:, js] = part * scale

        tile_terms(row_pts, col_pts, lambda row, col, width: delta_ref[pl.ds(row, PIECE), pl.ds(col, width)], *rest, False, emit)
        for ref, which in ((keep_ref, a), (send_ref, 1 - a)):
            ref[...] = result[:, pl.ds(pl.multiple_of(which * half, LANES), half)]

    scratch = [pltpu.VMEM((dims, cols), f32)] + tile_scratch(dims, rows, cols)
    outs = [(dims, half)] * 2
    return call(body, "tile_first", outs, scratch, tile_cost(rows, cols), delta, own, got, passed)


def open_tile(side_of, delta, rows_in, kept, passed, norm):
    dims, rows = rows_in.shape
    cols = delta.shape[1]
    half = cols // 2

    def body(delta_ref, rows_ref, kept_ref, passed_ref, norm_ref, part_ref, sums_ref, row_pts, col_pts, *rest):
        a = lax.axis_index("aux")
        at = lambda which: pl.ds(pl.multiple_of(which * half, LANES), half)
        base = side_of() * rows
        row_pts[...] = rows_ref[...]
        col_pts[:, at(a)] = kept_ref[...]
        col_pts[:, at(1 - a)] = passed_ref[...]

        def delta_at(row, col, width):
            return delta_ref[pl.ds(pl.multiple_of(base + row, PIECE), PIECE), pl.ds(col, width)]

        def emit(js, part):
            part_ref[:, js] = part

        misfit = tile_terms(row_pts, col_pts, delta_at, *rest, True, emit)
        sums_ref[:8] = jnp.full((8, LANES), misfit)
        sums_ref[8:] = norm_ref[...]

    outs = [(dims, cols), (SUMS, LANES)]
    scratch = tile_scratch(dims, rows, cols)
    return call(body, "tile_open", outs, scratch, tile_cost(rows, cols), delta, rows_in, kept, passed, norm)


def close_tile(side_of, which_of, scale, delta, rows_in, columns, part, sums):
    dims, rows = rows_in.shape
    half = columns.shape[1]

    def body(delta_ref, rows_ref, columns_ref, part_ref, sums_ref, out_ref, out_sums_ref, row_pts, col_pts, *rest):
        base = side_of() * rows
        first = which_of() * half
        row_pts[...] = rows_ref[...]
        col_pts[...] = columns_ref[...]

        def delta_at(row, col, width):
            return delta_ref[
                pl.ds(pl.multiple_of(base + row, PIECE), PIECE), pl.ds(pl.multiple_of(first + col, LANES), width)
            ]

        def emit(js, new):
            before = part_ref[:, pl.ds(pl.multiple_of(first + js.start, LANES), js.size)]
            out_ref[:, js] = (before + new) * scale

        misfit = tile_terms(row_pts, col_pts, delta_at, *rest, True, emit)
        out_sums_ref[:8] = sums_ref[:8] + misfit
        out_sums_ref[8:] = sums_ref[8:]

    outs = [(dims, half), (SUMS, LANES)]
    scratch = tile_scratch(dims, rows, half, rows, half)
    return call(body, "tile_close", outs, scratch, tile_cost(rows, half), delta, rows_in, columns, part, sums)


def norm_body(delta_ref, out_ref):
    rows, cols = delta_ref.shape
    total = jnp.zeros((8, LANES), f32)
    for ic in range(rows // LANES):
        for jc in range(cols // LANES):
            part = delta_ref[ic * LANES:(ic + 1) * LANES, jc * LANES:(jc + 1) * LANES].astype(f32)
            total = total + jnp.sum((part * part).reshape(LANES // 8, 8, LANES), axis=0)
    out_ref[...] = jnp.full((8, LANES), jnp.sum(total))


def norm_call(delta):
    return call(norm_body, "norm", [(8, LANES)], [], (4 * delta.size, 2 * delta.size, 0), delta)[0]


def stress_body(mine_ref, other_ref, out_ref):
    total = mine_ref[...] + other_ref[...]
    out_ref[0] = (total[:8] / total[8:])[0, 0]


def stress_call(mine, other):
    vmem = pl.BlockSpec(memory_space=pltpu.VMEM)
    return pl.pallas_call(
        stress_body,
        out_shape=jax.ShapeDtypeStruct((1,), f32),
        in_specs=[vmem] * 2,
        out_specs=pl.BlockSpec(memory_space=pltpu.SMEM),
        compiler_params=pltpu.CompilerParams(vmem_limit_bytes=40 << 20),
        name="stress",
    )(mine, other)


class Grid:
    def __init__(self):
        self.narrow = lax.axis_size("narrow")
        self.wide = lax.axis_size("wide")
        assert lax.axis_size("aux") == 2 and self.wide == 2 * self.narrow

    def pairs(self, source):
        place = lambda x, a, z: (z * self.narrow + x) * 2 + a
        return [
            (place(*source(x, a, z)), place(x, a, z))
            for z in range(self.wide)
            for x in range(self.narrow)
            for a in range(2)
        ]

    def send(self, value, source):
        return lax.ppermute(value, AXES, self.pairs(source))

    def other_core(self, value):
        return lax.ppermute(value, "aux", [(0, 1), (1, 0)])

    def across(self, value, axis, bit):
        return lax.ppermute(value, axis, [(i, i ^ bit) for i in range(lax.axis_size(axis))])

    def spread(self, late, flip=0):
        def source(x, a, z):
            block = 2 * x + a
            offset = z ^ block
            top, low = offset // self.narrow, offset % self.narrow
            if late:
                return x ^ low ^ (1 - top), a ^ top, block
            return x ^ low ^ flip, a ^ (1 - top), block

        return source

    def early(self, value):
        return self.send(value, self.spread(False)), self.send(value, self.spread(False, 1))

    def spread_half(self):
        x, a, z = (lax.axis_index(n) for n in ("narrow", "aux", "wide"))
        return a ^ 1 ^ ((z ^ (2 * x + a)) >> (self.narrow.bit_length() - 1))


def bits(count):
    return [1 << k for k in range(count.bit_length() - 1)]


def first_columns(grid, own):
    x, a, z = (lax.axis_index(n) for n in ("narrow", "aux", "wide"))
    current = own
    steps = bits(grid.narrow)
    for place, bit in enumerate(reversed(steps)):

        def source(x, a, z):
            return (x ^ bit, a, z) if a == z % 2 else (x, 1 - a, z ^ 1)

        got = grid.send(current, source)
        if place < len(steps) - 1:
            rest = (x ^ (z // 2)) & (2 * bit - 1)
            current = jnp.where((rest == bit) & (a == z % 2), got, current)
        elif len(steps) > 1:
            rest = (x ^ (z // 2)) & (2 * bit - 1)
            got = jnp.where(rest == bit, got, current)
    return got


def shards(dissimilarity, config):
    grid = Grid()
    cols = dissimilarity.shape[1]
    scale = 1.0 / (cols * grid.wide)
    own = config.T
    got = first_columns(grid, own)
    got, norm = lax.optimization_barrier((got, norm_call(dissimilarity)))
    passed = grid.other_core(got)

    keep, send = first_tile(grid.narrow, scale, dissimilarity, own, got, passed)
    half = keep + grid.other_core(send)
    for bit in bits(grid.narrow)[1:]:
        half = half + grid.across(half, "narrow", bit)
    first = grid.early(half)
    half = half + grid.across(half, "narrow", 1)
    first = first[0] + first[1]
    second = grid.send(half, grid.spread(True))
    other = grid.other_core(half)
    part, sums = open_tile(grid.spread_half, dissimilarity, first, half, other, norm)
    late = lambda: 1 - grid.spread_half()
    mine = lambda: lax.axis_index("aux")
    send, sums = close_tile(late, lambda: 1 - mine(), scale, dissimilarity, second, other, part, sums)
    keep, sums = close_tile(late, mine, scale, dissimilarity, second, half, part, sums)

    half = keep + grid.other_core(send)
    if grid.wide == 4:
        across = [grid.send(sums, lambda x, a, z, m=m, n=n: (x ^ m, a, z ^ n)) for m, n in ((0, 2), (1, 2), (1, 0))]
        sums = sums + across[0] + across[1] + across[2]
    else:
        for bit in bits(grid.narrow):
            sums = sums + grid.across(sums, "narrow", bit)
        for bit in bits(grid.wide)[1:]:
            sums = sums + grid.across(sums, "wide", bit)
    for bit in bits(grid.narrow):
        half = half + grid.across(half, "narrow", bit)
    first = grid.send(half, grid.spread(False))
    second = grid.send(half, grid.spread(True))
    sums = sums + grid.other_core(sums)
    stress = stress_call(sums, grid.across(sums, "wide", 1))
    first, second, stress = lax.optimization_barrier((first, second, stress))
    in_order = grid.spread_half() == 0
    embedding = jnp.where(
        in_order, jnp.concatenate([first, second], axis=1), jnp.concatenate([second, first], axis=1)
    )
    return embedding.T, stress


def solution(mesh):
    placed = (P(("groups", "narrow", "aux"), "wide"), P(("groups", "narrow", "aux"), None))
    return jax.shard_map(
        shards,
        mesh=mesh,
        in_specs=placed,
        out_specs=(P(("groups", "narrow", "aux"), None), P("groups")),
        check_vma=False,
    )
```

```python
import functools

import jax
import jax.numpy as jnp
from jax import lax
from jax.experimental import pallas as pl
from jax.experimental.pallas import tpu as pltpu
from jax.sharding import PartitionSpec as P

FLOOR = 3.0
TINY = 1e-30
DEPTH = 256
LANES = 128
EXTRA = 16
PIECE = 32
SUMS = 16

f32 = jnp.float32
bf16 = jnp.bfloat16
AXES = ("wide", "narrow", "aux")


def split2(values):
    high = values.astype(bf16)
    return high, (values - high.astype(f32)).astype(bf16)


def split3(values):
    high = values.astype(bf16)
    rest = values - high.astype(f32)
    middle = rest.astype(bf16)
    return high, middle, (rest - middle.astype(f32)).astype(bf16)


def norm_rows(points, first):
    count = points.shape[1]
    squares = jnp.sum(points * points, axis=0, keepdims=True)
    row = lax.broadcasted_iota(jnp.int32, (EXTRA, count), 0)
    ones = 3 if first else 0
    parts = 0 if first else 3
    rows = jnp.where((row >= ones) & (row < ones + 3), 1.0, 0.0)
    for k, part in enumerate(split3(squares)):
        rows = jnp.where(row == parts + k, part.astype(f32), rows)
    return rows.astype(bf16)


def tile_terms(row_pts, col_pts, delta_at, lhs, rhs, left, square, r_both, stress, emit):
    dims, rows = row_pts.shape
    cols = col_pts.shape[1]
    step = r_both.shape[2]
    points = row_pts[...]
    shift = jnp.sum(points, axis=1, keepdims=True) * (1.0 / rows)
    points = points - shift
    high, middle = split2(points)
    minus2 = lambda v: (v.astype(f32) * -2.0).astype(bf16)
    fill = DEPTH - 3 * dims - EXTRA
    lhs[...] = jnp.concatenate(
        [minus2(high), minus2(high), minus2(middle), norm_rows(points, True), jnp.zeros((fill, rows), bf16)], axis=0
    ).T
    factors = jnp.concatenate([high, middle, jnp.ones((EXTRA, rows), bf16)], axis=0)
    tall = r_both.shape[1] // 2
    for row in range(0, rows, tall):
        left[:, 2 * row:2 * row + tall] = factors[:, row:row + tall]
        left[:, 2 * row + tall:2 * (row + tall)] = factors[:, row:row + tall]
    points = col_pts[...] - shift
    col_pts[...] = points
    high, middle = split2(points)
    rhs[...] = jnp.concatenate(
        [high, middle, high, norm_rows(points, False), jnp.zeros((fill, cols), bf16)], axis=0
    )

    units = [(row, col) for col in range(0, cols, step) for row in range(0, rows, tall)]

    def gram(u):
        row, col = units[u]
        square[u % 2] = jnp.dot(lhs[row:row + tall, :], rhs[:, col:col + step], preferred_element_type=f32)

    misfit = jnp.zeros((16, step), f32)
    terms = None
    gram(0)
    for u, (row, col) in enumerate(units):
        if u + 1 < len(units):
            gram(u + 1)
        slot = u % 2
        for p in range(0, tall, PIECE):
            squared = square[slot, p:p + PIECE, :]
            delta = delta_at(row + p, col, step).astype(f32)
            if stress:
                inverse = lax.rsqrt(jnp.maximum(squared, TINY))
                ratio = delta * jnp.minimum(inverse, 1.0 / FLOOR)
                gap = delta - jnp.maximum(squared, 0.0) * inverse
                gap = gap * gap
                for q in range(0, PIECE, 16):
                    misfit = misfit + gap[q:q + 16]
            else:
                ratio = delta * lax.rsqrt(jnp.maximum(squared, FLOOR * FLOOR))
            high, low = split2(ratio)
            r_both[slot, p:p + PIECE, :] = high
            r_both[slot, tall + p:tall + p + PIECE, :] = low
        part = jnp.dot(left[:, 2 * row:2 * (row + tall)], r_both[slot], preferred_element_type=f32)
        terms = part if terms is None else terms + part
        if row + tall == rows:
            cross = terms[:dims] + terms[dims:2 * dims]
            js = pl.ds(col, step)
            emit(js, col_pts[:, js] * terms[2 * dims:2 * dims + 1] - cross)
            terms = None
    return jnp.sum(misfit) if stress else None


def tile_scratch(dims, rows, cols, tall=None, step=None):
    tall = tall or rows
    step = step or (256 if cols % 256 == 0 else LANES)
    return [
        pltpu.VMEM((dims, rows), f32),
        pltpu.VMEM((dims, cols), f32),
        pltpu.VMEM((rows, DEPTH), bf16),
        pltpu.VMEM((DEPTH, cols), bf16),
        pltpu.VMEM((2 * dims + EXTRA, 2 * rows), bf16),
        pltpu.VMEM((2, tall, step), f32),
        pltpu.VMEM((2, 2 * tall, step), bf16),
    ]


def call(body, name, outs, scratch, cost, *arrays):
    vmem = pl.BlockSpec(memory_space=pltpu.VMEM)
    flops, size, roots = cost
    return pl.pallas_call(
        body,
        out_shape=[jax.ShapeDtypeStruct(shape, f32) for shape in outs],
        in_specs=[vmem] * len(arrays),
        out_specs=[vmem] * len(outs),
        scratch_shapes=scratch,
        compiler_params=pltpu.CompilerParams(vmem_limit_bytes=40 << 20),
        cost_estimate=pl.CostEstimate(flops=flops, bytes_accessed=size, transcendentals=roots),
        name=name,
    )(*arrays)


def tile_cost(rows, cols):
    return 2 * 3 * rows * cols * DEPTH, 2 * rows * cols, rows * cols


def first_tile(narrow, scale, delta, own, got, passed):
    dims, rows = own.shape
    cols = delta.shape[1]
    half = cols // 2

    def body(delta_ref, own_ref, got_ref, passed_ref, keep_ref, send_ref, result, row_pts, col_pts, *rest):
        x, a, z = (lax.axis_index(n) for n in ("narrow", "aux", "wide"))
        home = (x == z // 2) & (narrow == 2)
        core = a == z % 2
        row_pts[...] = own_ref[...]

        @pl.when(home & core)
        def _():
            col_pts[...] = own_ref[...]

        @pl.when(home != core)
        def _():
            col_pts[...] = got_ref[...]

        @pl.when(jnp.logical_not(home | core))
        def _():
            col_pts[...] = passed_ref[...]

        def emit(js, part):
            result[:, js] = part * scale

        tile_terms(row_pts, col_pts, lambda row, col, width: delta_ref[pl.ds(row, PIECE), pl.ds(col, width)], *rest, False, emit)
        for ref, which in ((keep_ref, a), (send_ref, 1 - a)):
            ref[...] = result[:, pl.ds(pl.multiple_of(which * half, LANES), half)]

    scratch = [pltpu.VMEM((dims, cols), f32)] + tile_scratch(dims, rows, cols)
    outs = [(dims, half)] * 2
    return call(body, "tile_first", outs, scratch, tile_cost(rows, cols), delta, own, got, passed)


def open_tile(side_of, delta, rows_in, kept, passed, norm):
    dims, rows = rows_in.shape
    cols = delta.shape[1]
    half = cols // 2

    def body(delta_ref, rows_ref, kept_ref, passed_ref, norm_ref, part_ref, sums_ref, row_pts, col_pts, *rest):
        a = lax.axis_index("aux")
        at = lambda which: pl.ds(pl.multiple_of(which * half, LANES), half)
        base = side_of() * rows
        row_pts[...] = rows_ref[...]
        col_pts[:, at(a)] = kept_ref[...]
        col_pts[:, at(1 - a)] = passed_ref[...]

        def delta_at(row, col, width):
            return delta_ref[pl.ds(pl.multiple_of(base + row, PIECE), PIECE), pl.ds(col, width)]

        def emit(js, part):
            part_ref[:, js] = part

        misfit = tile_terms(row_pts, col_pts, delta_at, *rest, True, emit)
        sums_ref[:8] = jnp.full((8, LANES), misfit)
        sums_ref[8:] = norm_ref[...]

    outs = [(dims, cols), (SUMS, LANES)]
    scratch = tile_scratch(dims, rows, cols, rows, cols // 2)
    return call(body, "tile_open", outs, scratch, tile_cost(rows, cols), delta, rows_in, kept, passed, norm)


def close_tile(side_of, which_of, scale, delta, rows_in, columns, part, sums):
    dims, rows = rows_in.shape
    half = columns.shape[1]

    def body(delta_ref, rows_ref, columns_ref, part_ref, sums_ref, out_ref, out_sums_ref, row_pts, col_pts, *rest):
        base = side_of() * rows
        first = which_of() * half
        row_pts[...] = rows_ref[...]
        col_pts[...] = columns_ref[...]

        def delta_at(row, col, width):
            return delta_ref[
                pl.ds(pl.multiple_of(base + row, PIECE), PIECE), pl.ds(pl.multiple_of(first + col, LANES), width)
            ]

        def emit(js, new):
            before = part_ref[:, pl.ds(pl.multiple_of(first + js.start, LANES), js.size)]
            out_ref[:, js] = (before + new) * scale

        misfit = tile_terms(row_pts, col_pts, delta_at, *rest, True, emit)
        out_sums_ref[:8] = sums_ref[:8] + misfit
        out_sums_ref[8:] = sums_ref[8:]

    outs = [(dims, half), (SUMS, LANES)]
    scratch = tile_scratch(dims, rows, half, rows, half)
    return call(body, "tile_close", outs, scratch, tile_cost(rows, half), delta, rows_in, columns, part, sums)


def norm_body(delta_ref, out_ref):
    rows, cols = delta_ref.shape
    total = jnp.zeros((8, LANES), f32)
    for ic in range(rows // LANES):
        for jc in range(cols // LANES):
            part = delta_ref[ic * LANES:(ic + 1) * LANES, jc * LANES:(jc + 1) * LANES].astype(f32)
            total = total + jnp.sum((part * part).reshape(LANES // 8, 8, LANES), axis=0)
    out_ref[...] = jnp.full((8, LANES), jnp.sum(total))


def norm_call(delta):
    return call(norm_body, "norm", [(8, LANES)], [], (4 * delta.size, 2 * delta.size, 0), delta)[0]


def stress_body(mine_ref, other_ref, out_ref):
    total = mine_ref[...] + other_ref[...]
    out_ref[0] = (total[:8] / total[8:])[0, 0]


def stress_call(mine, other):
    vmem = pl.BlockSpec(memory_space=pltpu.VMEM)
    return pl.pallas_call(
        stress_body,
        out_shape=jax.ShapeDtypeStruct((1,), f32),
        in_specs=[vmem] * 2,
        out_specs=pl.BlockSpec(memory_space=pltpu.SMEM),
        compiler_params=pltpu.CompilerParams(vmem_limit_bytes=40 << 20),
        name="stress",
    )(mine, other)


class Grid:
    def __init__(self):
        self.narrow = lax.axis_size("narrow")
        self.wide = lax.axis_size("wide")
        assert lax.axis_size("aux") == 2 and self.wide == 2 * self.narrow

    def pairs(self, source):
        place = lambda x, a, z: (z * self.narrow + x) * 2 + a
        return [
            (place(*source(x, a, z)), place(x, a, z))
            for z in range(self.wide)
            for x in range(self.narrow)
            for a in range(2)
        ]

    def send(self, value, source):
        return lax.ppermute(value, AXES, self.pairs(source))

    def other_core(self, value):
        return lax.ppermute(value, "aux", [(0, 1), (1, 0)])

    def across(self, value, axis, bit):
        return lax.ppermute(value, axis, [(i, i ^ bit) for i in range(lax.axis_size(axis))])

    def spread(self, late, flip=0):
        def source(x, a, z):
            block = 2 * x + a
            offset = z ^ block
            top, low = offset // self.narrow, offset % self.narrow
            if late:
                return x ^ low ^ (1 - top), a ^ top, block
            return x ^ low ^ flip, a ^ (1 - top), block

        return source

    def early(self, value):
        return self.send(value, self.spread(False)), self.send(value, self.spread(False, 1))

    def spread_half(self):
        x, a, z = (lax.axis_index(n) for n in ("narrow", "aux", "wide"))
        return a ^ 1 ^ ((z ^ (2 * x + a)) >> (self.narrow.bit_length() - 1))


def bits(count):
    return [1 << k for k in range(count.bit_length() - 1)]


def first_columns(grid, own):
    x, a, z = (lax.axis_index(n) for n in ("narrow", "aux", "wide"))
    current = own
    steps = bits(grid.narrow)
    for place, bit in enumerate(reversed(steps)):

        def source(x, a, z):
            return (x ^ bit, a, z) if a == z % 2 else (x, 1 - a, z ^ 1)

        got = grid.send(current, source)
        if place < len(steps) - 1:
            rest = (x ^ (z // 2)) & (2 * bit - 1)
            current = jnp.where((rest == bit) & (a == z % 2), got, current)
        elif len(steps) > 1:
            rest = (x ^ (z // 2)) & (2 * bit - 1)
            got = jnp.where(rest == bit, got, current)
    return got


def shards(dissimilarity, config):
    grid = Grid()
    cols = dissimilarity.shape[1]
    scale = 1.0 / (cols * grid.wide)
    own = config.T
    got = first_columns(grid, own)
    got, norm = lax.optimization_barrier((got, norm_call(dissimilarity)))
    passed = grid.other_core(got)

    keep, send = first_tile(grid.narrow, scale, dissimilarity, own, got, passed)
    half = keep + grid.other_core(send)
    for bit in bits(grid.narrow)[1:]:
        half = half + grid.across(half, "narrow", bit)
    first = grid.early(half)
    half = half + grid.across(half, "narrow", 1)
    first = first[0] + first[1]
    second = grid.send(half, grid.spread(True))
    other = grid.other_core(half)
    part, sums = open_tile(grid.spread_half, dissimilarity, first, half, other, norm)
    late = lambda: 1 - grid.spread_half()
    mine = lambda: lax.axis_index("aux")
    send, sums = close_tile(late, lambda: 1 - mine(), scale, dissimilarity, second, other, part, sums)
    keep, sums = close_tile(late, mine, scale, dissimilarity, second, half, part, sums)

    half = keep + grid.other_core(send)
    if grid.wide == 4:
        across = [grid.send(sums, lambda x, a, z, m=m, n=n: (x ^ m, a, z ^ n)) for m, n in ((0, 2), (1, 2), (1, 0))]
        sums = sums + across[0] + across[1] + across[2]
    else:
        for bit in bits(grid.narrow):
            sums = sums + grid.across(sums, "narrow", bit)
        for bit in bits(grid.wide)[1:]:
            sums = sums + grid.across(sums, "wide", bit)
    for bit in bits(grid.narrow):
        half = half + grid.across(half, "narrow", bit)
    first = grid.send(half, grid.spread(False))
    second = grid.send(half, grid.spread(True))
    sums = sums + grid.other_core(sums)
    stress = stress_call(sums, grid.across(sums, "wide", 1))
    first, second, stress = lax.optimization_barrier((first, second, stress))
    in_order = grid.spread_half() == 0
    embedding = jnp.where(
        in_order, jnp.concatenate([first, second], axis=1), jnp.concatenate([second, first], axis=1)
    )
    return embedding.T, stress


def solution(mesh):
    placed = (P(("groups", "narrow", "aux"), "wide"), P(("groups", "narrow", "aux"), None))
    return jax.shard_map(
        shards,
        mesh=mesh,
        in_specs=placed,
        out_specs=(P(("groups", "narrow", "aux"), None), P("groups")),
        check_vma=False,
    )
```

```python
import functools

import jax
import jax.numpy as jnp
from jax import lax
from jax.experimental import pallas as pl
from jax.experimental.pallas import tpu as pltpu
from jax.sharding import PartitionSpec as P

FLOOR = 3.0
TINY = 1e-30
DEPTH = 256
LANES = 128
EXTRA = 16
PIECE = 32
SUMS = 16

f32 = jnp.float32
bf16 = jnp.bfloat16
AXES = ("wide", "narrow", "aux")


def split2(values):
    high = values.astype(bf16)
    return high, (values - high.astype(f32)).astype(bf16)


def split3(values):
    high = values.astype(bf16)
    rest = values - high.astype(f32)
    middle = rest.astype(bf16)
    return high, middle, (rest - middle.astype(f32)).astype(bf16)


def norm_rows(points, first):
    count = points.shape[1]
    squares = jnp.sum(points * points, axis=0, keepdims=True)
    row = lax.broadcasted_iota(jnp.int32, (EXTRA, count), 0)
    ones = 3 if first else 0
    parts = 0 if first else 3
    rows = jnp.where((row >= ones) & (row < ones + 3), 1.0, 0.0)
    for k, part in enumerate(split3(squares)):
        rows = jnp.where(row == parts + k, part.astype(f32), rows)
    return rows.astype(bf16)


def tile_terms(row_pts, col_pts, delta_at, lhs, rhs, left, square, r_both, stress, emit):
    dims, rows = row_pts.shape
    cols = col_pts.shape[1]
    step = r_both.shape[2]
    points = row_pts[...]
    shift = jnp.sum(points, axis=1, keepdims=True) * (1.0 / rows)
    points = points - shift
    high, middle = split2(points)
    minus2 = lambda v: (v.astype(f32) * -2.0).astype(bf16)
    fill = DEPTH - 3 * dims - EXTRA
    lhs[...] = jnp.concatenate(
        [minus2(high), minus2(high), minus2(middle), norm_rows(points, True), jnp.zeros((fill, rows), bf16)], axis=0
    ).T
    factors = jnp.concatenate([high, middle, jnp.ones((EXTRA, rows), bf16)], axis=0)
    tall = r_both.shape[1] // 2
    for row in range(0, rows, tall):
        left[:, 2 * row:2 * row + tall] = factors[:, row:row + tall]
        left[:, 2 * row + tall:2 * (row + tall)] = factors[:, row:row + tall]
    points = col_pts[...] - shift
    col_pts[...] = points
    high, middle = split2(points)
    rhs[...] = jnp.concatenate(
        [high, middle, high, norm_rows(points, False), jnp.zeros((fill, cols), bf16)], axis=0
    )

    units = [(row, col) for col in range(0, cols, step) for row in range(0, rows, tall)]

    def gram(u):
        row, col = units[u]
        square[u % 2] = jnp.dot(lhs[row:row + tall, :], rhs[:, col:col + step], preferred_element_type=f32)

    misfit = jnp.zeros((16, step), f32)
    terms = None
    gram(0)
    for u, (row, col) in enumerate(units):
        if u + 1 < len(units):
            gram(u + 1)
        slot = u % 2
        for p in range(0, tall, PIECE):
            squared = square[slot, p:p + PIECE, :]
            delta = delta_at(row + p, col, step).astype(f32)
            if stress:
                inverse = lax.rsqrt(jnp.maximum(squared, TINY))
                ratio = delta * jnp.minimum(inverse, 1.0 / FLOOR)
                gap = delta - jnp.maximum(squared, 0.0) * inverse
                gap = gap * gap
                for q in range(0, PIECE, 16):
                    misfit = misfit + gap[q:q + 16]
            else:
                ratio = delta * lax.rsqrt(jnp.maximum(squared, FLOOR * FLOOR))
            high, low = split2(ratio)
            r_both[slot, p:p + PIECE, :] = high
            r_both[slot, tall + p:tall + p + PIECE, :] = low
        part = jnp.dot(left[:, 2 * row:2 * (row + tall)], r_both[slot], preferred_element_type=f32)
        terms = part if terms is None else terms + part
        if row + tall == rows:
            cross = terms[:dims] + terms[dims:2 * dims]
            js = pl.ds(col, step)
            emit(js, col_pts[:, js] * terms[2 * dims:2 * dims + 1] - cross)
            terms = None
    return jnp.sum(misfit) if stress else None


def tile_scratch(dims, rows, cols, tall=None, step=None):
    tall = tall or rows
    step = step or (256 if cols % 256 == 0 else LANES)
    return [
        pltpu.VMEM((dims, rows), f32),
        pltpu.VMEM((dims, cols), f32),
        pltpu.VMEM((rows, DEPTH), bf16),
        pltpu.VMEM((DEPTH, cols), bf16),
        pltpu.VMEM((2 * dims + EXTRA, 2 * rows), bf16),
        pltpu.VMEM((2, tall, step), f32),
        pltpu.VMEM((2, 2 * tall, step), bf16),
    ]


def call(body, name, outs, scratch, cost, *arrays):
    vmem = pl.BlockSpec(memory_space=pltpu.VMEM)
    flops, size, roots = cost
    return pl.pallas_call(
        body,
        out_shape=[jax.ShapeDtypeStruct(shape, f32) for shape in outs],
        in_specs=[vmem] * len(arrays),
        out_specs=[vmem] * len(outs),
        scratch_shapes=scratch,
        compiler_params=pltpu.CompilerParams(vmem_limit_bytes=40 << 20),
        cost_estimate=pl.CostEstimate(flops=flops, bytes_accessed=size, transcendentals=roots),
        name=name,
    )(*arrays)


def tile_cost(rows, cols):
    return 2 * 3 * rows * cols * DEPTH, 2 * rows * cols, rows * cols


def first_tile(narrow, scale, delta, own, got, passed):
    dims, rows = own.shape
    cols = delta.shape[1]
    half = cols // 2

    def body(delta_ref, own_ref, got_ref, passed_ref, keep_ref, send_ref, result, row_pts, col_pts, *rest):
        x, a, z = (lax.axis_index(n) for n in ("narrow", "aux", "wide"))
        home = (x == z // 2) & (narrow == 2)
        core = a == z % 2
        row_pts[...] = own_ref[...]

        @pl.when(home & core)
        def _():
            col_pts[...] = own_ref[...]

        @pl.when(home != core)
        def _():
            col_pts[...] = got_ref[...]

        @pl.when(jnp.logical_not(home | core))
        def _():
            col_pts[...] = passed_ref[...]

        def emit(js, part):
            result[:, js] = part * scale

        tile_terms(row_pts, col_pts, lambda row, col, width: delta_ref[pl.ds(row, PIECE), pl.ds(col, width)], *rest, False, emit)
        for ref, which in ((keep_ref, a), (send_ref, 1 - a)):
            ref[...] = result[:, pl.ds(pl.multiple_of(which * half, LANES), half)]

    scratch = [pltpu.VMEM((dims, cols), f32)] + tile_scratch(dims, rows, cols)
    outs = [(dims, half)] * 2
    return call(body, "tile_first", outs, scratch, tile_cost(rows, cols), delta, own, got, passed)


def open_tile(side_of, delta, rows_in, kept, passed, norm):
    dims, rows = rows_in.shape
    cols = delta.shape[1]
    half = cols // 2

    def body(delta_ref, rows_ref, kept_ref, passed_ref, norm_ref, part_ref, sums_ref, row_pts, col_pts, *rest):
        a = lax.axis_index("aux")
        at = lambda which: pl.ds(pl.multiple_of(which * half, LANES), half)
        base = side_of() * rows
        row_pts[...] = rows_ref[...]
        col_pts[:, at(a)] = kept_ref[...]
        col_pts[:, at(1 - a)] = passed_ref[...]

        def delta_at(row, col, width):
            return delta_ref[pl.ds(pl.multiple_of(base + row, PIECE), PIECE), pl.ds(col, width)]

        def emit(js, part):
            part_ref[:, js] = part

        misfit = tile_terms(row_pts, col_pts, delta_at, *rest, True, emit)
        sums_ref[:8] = jnp.full((8, LANES), misfit)
        sums_ref[8:] = norm_ref[...]

    outs = [(dims, cols), (SUMS, LANES)]
    scratch = tile_scratch(dims, rows, cols)
    return call(body, "tile_open", outs, scratch, tile_cost(rows, cols), delta, rows_in, kept, passed, norm)


def close_tile(side_of, which_of, scale, delta, rows_in, columns, part, sums):
    dims, rows = rows_in.shape
    half = columns.shape[1]

    def body(delta_ref, rows_ref, columns_ref, part_ref, sums_ref, out_ref, out_sums_ref, row_pts, col_pts, *rest):
        base = side_of() * rows
        first = which_of() * half
        row_pts[...] = rows_ref[...]
        col_pts[...] = columns_ref[...]

        def delta_at(row, col, width):
            return delta_ref[
                pl.ds(pl.multiple_of(base + row, PIECE), PIECE), pl.ds(pl.multiple_of(first + col, LANES), width)
            ]

        def emit(js, new):
            before = part_ref[:, pl.ds(pl.multiple_of(first + js.start, LANES), js.size)]
            out_ref[:, js] = (before + new) * scale

        misfit = tile_terms(row_pts, col_pts, delta_at, *rest, True, emit)
        out_sums_ref[:8] = sums_ref[:8] + misfit
        out_sums_ref[8:] = sums_ref[8:]

    outs = [(dims, half), (SUMS, LANES)]
    scratch = tile_scratch(dims, rows, half, rows, half)
    return call(body, "tile_close", outs, scratch, tile_cost(rows, half), delta, rows_in, columns, part, sums)


def norm_body(delta_ref, out_ref):
    rows, cols = delta_ref.shape
    total = jnp.zeros((8, LANES), f32)
    for ic in range(rows // LANES):
        for jc in range(cols // LANES):
            part = delta_ref[ic * LANES:(ic + 1) * LANES, jc * LANES:(jc + 1) * LANES].astype(f32)
            total = total + jnp.sum((part * part).reshape(LANES // 8, 8, LANES), axis=0)
    out_ref[...] = jnp.full((8, LANES), jnp.sum(total))


def norm_call(delta):
    return call(norm_body, "norm", [(8, LANES)], [], (4 * delta.size, 2 * delta.size, 0), delta)[0]


def stress_body(mine_ref, other_ref, out_ref):
    total = mine_ref[...] + other_ref[...]
    out_ref[0] = (total[:8] / total[8:])[0, 0]


def stress_call(mine, other):
    vmem = pl.BlockSpec(memory_space=pltpu.VMEM)
    return pl.pallas_call(
        stress_body,
        out_shape=jax.ShapeDtypeStruct((1,), f32),
        in_specs=[vmem] * 2,
        out_specs=pl.BlockSpec(memory_space=pltpu.SMEM),
        compiler_params=pltpu.CompilerParams(vmem_limit_bytes=40 << 20),
        name="stress",
    )(mine, other)


class Grid:
    def __init__(self):
        self.narrow = lax.axis_size("narrow")
        self.wide = lax.axis_size("wide")
        assert lax.axis_size("aux") == 2 and self.wide == 2 * self.narrow

    def pairs(self, source):
        place = lambda x, a, z: (z * self.narrow + x) * 2 + a
        return [
            (place(*source(x, a, z)), place(x, a, z))
            for z in range(self.wide)
            for x in range(self.narrow)
            for a in range(2)
        ]

    def send(self, value, source):
        return lax.ppermute(value, AXES, self.pairs(source))

    def other_core(self, value):
        return lax.ppermute(value, "aux", [(0, 1), (1, 0)])

    def across(self, value, axis, bit):
        return lax.ppermute(value, axis, [(i, i ^ bit) for i in range(lax.axis_size(axis))])

    def spread(self, late, flip=0):
        def source(x, a, z):
            block = 2 * x + a
            offset = z ^ block
            top, low = offset // self.narrow, offset % self.narrow
            if late:
                return x ^ low ^ (1 - top), a ^ top, block
            return x ^ low ^ flip, a ^ (1 - top), block

        return source

    def early(self, value):
        return self.send(value, self.spread(False)), self.send(value, self.spread(False, 1))

    def spread_half(self):
        x, a, z = (lax.axis_index(n) for n in ("narrow", "aux", "wide"))
        return a ^ 1 ^ ((z ^ (2 * x + a)) >> (self.narrow.bit_length() - 1))


def bits(count):
    return [1 << k for k in range(count.bit_length() - 1)]


def first_columns(grid, own):
    x, a, z = (lax.axis_index(n) for n in ("narrow", "aux", "wide"))
    current = own
    steps = bits(grid.narrow)
    for place, bit in enumerate(reversed(steps)):

        def source(x, a, z):
            return (x ^ bit, a, z) if a == z % 2 else (x, 1 - a, z ^ 1)

        got = grid.send(current, source)
        if place < len(steps) - 1:
            rest = (x ^ (z // 2)) & (2 * bit - 1)
            current = jnp.where((rest == bit) & (a == z % 2), got, current)
        elif len(steps) > 1:
            rest = (x ^ (z // 2)) & (2 * bit - 1)
            got = jnp.where(rest == bit, got, current)
    return got


def shards(dissimilarity, config):
    grid = Grid()
    cols = dissimilarity.shape[1]
    scale = 1.0 / (cols * grid.wide)
    own = config.T
    got = first_columns(grid, own)
    got, norm = lax.optimization_barrier((got, norm_call(dissimilarity)))
    passed = grid.other_core(got)

    keep, send = first_tile(grid.narrow, scale, dissimilarity, own, got, passed)
    half = keep + grid.other_core(send)
    for bit in bits(grid.narrow)[1:]:
        half = half + grid.across(half, "narrow", bit)
    first = grid.early(half)
    half = half + grid.across(half, "narrow", 1)
    first = first[0] + first[1]
    second = grid.send(half, grid.spread(True))
    other = grid.other_core(half)
    part, sums = open_tile(grid.spread_half, dissimilarity, first, half, other, norm)
    late = lambda: 1 - grid.spread_half()
    mine = lambda: lax.axis_index("aux")
    send, sums = close_tile(late, lambda: 1 - mine(), scale, dissimilarity, second, other, part, sums)
    keep, sums = close_tile(late, mine, scale, dissimilarity, second, half, part, sums)

    half = keep + grid.other_core(send)
    sums = sums + grid.other_core(sums)
    if grid.wide == 4:
        across = [grid.send(sums, lambda x, a, z, m=m, n=n: (x ^ m, a, z ^ n)) for m, n in ((0, 2), (1, 2), (1, 0))]
        sums = sums + across[0] + across[1] + across[2]
    else:
        for bit in bits(grid.narrow):
            sums = sums + grid.across(sums, "narrow", bit)
        for bit in bits(grid.wide)[1:]:
            sums = sums + grid.across(sums, "wide", bit)
    for bit in bits(grid.narrow):
        half = half + grid.across(half, "narrow", bit)
    first = grid.send(half, grid.spread(False))
    second = grid.send(half, grid.spread(True))
    stress = stress_call(sums, grid.across(sums, "wide", 1))
    first, second, stress = lax.optimization_barrier((first, second, stress))
    in_order = grid.spread_half() == 0
    embedding = jnp.where(
        in_order, jnp.concatenate([first, second], axis=1), jnp.concatenate([second, first], axis=1)
    )
    return embedding.T, stress


def solution(mesh):
    placed = (P(("groups", "narrow", "aux"), "wide"), P(("groups", "narrow", "aux"), None))
    return jax.shard_map(
        shards,
        mesh=mesh,
        in_specs=placed,
        out_specs=(P(("groups", "narrow", "aux"), None), P("groups")),
        check_vma=False,
    )
```
